32 devices in a mesh: tile: 4 (over y, core), plane: 8 (over z, x).
Axes of the slice: x: 2, y: 2, z: 4, core: 2. Of those that a mesh axis runs over, the one named last changes fastest.
Arguments:
- observed: float32 [2, 8, 256, 256], P(None, 'plane', 'tile'), may hold values from 0.5 to 4
- intersection_strip: float32 [2, 8, 128, 256], P(None, 'plane', 'tile'), may hold values from 0.5 to 4
- axial_taps: float32 [2, 41], replicated, may hold values from 0.05 to 1
- lateral_taps: float32 [2, 15], replicated, may hold values from 0.05 to 1
- extents: int32 [4], P('tile'), may hold values from 1 to 32, as said below
- section_skews: int32 [4], P('tile'), may hold values from 0 to 255
Outputs:
- estimate: float32 [2, 8, 256, 256], P(None, 'plane', 'tile')
The draws below stay inside these ranges and needn't reach their ends.
Inputs may be any that keep to these rules, and one draw needn't show every extreme that they name: `extents`: entry 0 is not used; the largest of the entries 1 to 3 is 32.
All inputs are finite; a program needn't handle non-finite values.
Results may differ from the reference program's by a relative error of at most 0.00005.
Values sent between devices are 32-bit elements; how exact they have to be, the bound alone decides.
No kernel may reach another device: no remote copies, remote signals or barrier semaphores. Data moves between devices by JAX's collectives and lax.ppermute only.
A program may use at most 64 MiB of HBM per device.

```python
import math
import jax
import jax.numpy as jnp
from jax import lax

CH = 2
KZ = 41
KL = 15
ITERS = 2
YD = 64
NX = 256
MAXOV = 32
TILES = 4
NZ = 8
NY = 256


def draw_extents(key, part):
    first_key, second_key = jax.random.split(jax.random.fold_in(key, 17))
    values = jax.random.randint(first_key, (TILES,), 1, MAXOV + 1)
    chosen = jax.random.randint(second_key, (), 1, TILES)
    return jnp.where(jnp.arange(TILES) == chosen, MAXOV, values).astype(jnp.int32)


def touch_ends(array, own_key, low, high):
    longest = array.shape.index(max(array.shape))
    spots = []
    for shift in (0, 1):
        where = [jax.random.randint(jax.random.fold_in(own_key, axis), (), 0, length) for axis, length in enumerate(array.shape)]
        where[longest] = (where[longest] + shift) % array.shape[longest]
        spots.append(tuple(where))
    return array.at[spots[0]].set(low).at[spots[1]].set(high)


def block_scale(key, dims, cuts, smallest, high):
    gain = 1.0
    for axis_at, shards_of in cuts:
        steps = jax.random.uniform(jax.random.fold_in(jax.random.fold_in(key, 6), axis_at), (shards_of,), jnp.float32, smallest / len(cuts), high / len(cuts))
        gain = gain * jnp.repeat(jnp.exp(steps), dims[axis_at] // shards_of).reshape((-1,) + (1,) * (len(dims) - 1 - axis_at))
    return gain


def setup_inputs(seed: int = 0) -> dict:
    key_of = jax.random.split(jax.random.key(seed), 7)
    return {
        "observed": jnp.clip(jnp.exp(math.log(4.0) - 2.0794415 * jax.random.uniform(key_of[0], (CH, NZ, NY, NX), jnp.float32) ** block_scale(key_of[0], (CH, NZ, NY, NX), ((1, 8), (2, 4)), -0.2, 0.2)), 0.5, 4.0),
        "intersection_strip": jnp.clip(jnp.exp(math.log(4.0) - 2.0794415 * jax.random.uniform(key_of[1], (CH, NZ, TILES * MAXOV, NX), jnp.float32) ** block_scale(key_of[1], (CH, NZ, TILES * MAXOV, NX), ((1, 8), (2, 4)), -0.2, 0.2)), 0.5, 4.0),
        "axial_taps": jnp.clip(jnp.exp(jax.random.uniform(key_of[2], (CH, KZ), jnp.float32, math.log(0.05), math.log(1.0))), 0.05, 1.0),
        "lateral_taps": jnp.clip(jnp.exp(jax.random.uniform(key_of[3], (CH, KL), jnp.float32, math.log(0.05), math.log(1.0))), 0.05, 1.0),
        "extents": draw_extents(jax.random.fold_in(key_of[6], 71), 0),
        "section_skews": touch_ends(jax.random.randint(key_of[5], (TILES,), 0, NX), jax.random.fold_in(key_of[5], 1), 0, NX - 1).astype(jnp.int32),
    }


def shifted_blur(volume, kernel, axis):
    tap_count = kernel.shape[0]
    half_width = tap_count // 2
    padding = [(0, 0)] * volume.ndim
    padding[axis] = (half_width, half_width)
    padded = jnp.pad(volume, padding)
    length_here = volume.shape[axis]
    running = jnp.zeros_like(volume)
    for tap_index in range(tap_count):
        running = running + kernel[tap_index] * lax.slice_in_dim(padded, tap_index, tap_index + length_here, axis=axis)
    return running


def one_channel(operands):
    joined_obs, axial_kernel, lateral_kernel = operands
    axial_flip = jnp.flip(axial_kernel)
    lateral_flip = jnp.flip(lateral_kernel)
    estimate = joined_obs
    for sweep in range(ITERS):
        blurred = shifted_blur(shifted_blur(shifted_blur(estimate, lateral_kernel, 2), lateral_kernel, 1), axial_kernel, 0)
        quotient = joined_obs / blurred
        spread_back = shifted_blur(shifted_blur(shifted_blur(quotient, axial_flip, 0), lateral_flip, 1), lateral_flip, 2)
        estimate = estimate * spread_back
    return estimate


def reference(observed, intersection_strip, axial_taps, lateral_taps, extents, section_skews):
    joined_obs = observed
    for tile_index in range(1, TILES):
        strip_part = intersection_strip[:, :, (tile_index - 1) * MAXOV:tile_index * MAXOV, :]
        strip_part = jnp.roll(strip_part, section_skews[tile_index], axis=3)
        top_rows = observed[:, :, tile_index * YD:tile_index * YD + MAXOV, :]
        inside = (jnp.arange(MAXOV, dtype=jnp.int32) < extents[tile_index])[None, None, :, None]
        blended = jnp.where(inside, 0.5 * (top_rows + strip_part), top_rows)
        joined_obs = joined_obs.at[:, :, tile_index * YD:tile_index * YD + MAXOV, :].set(blended)
    return lax.map(one_channel, (joined_obs, axial_taps, lateral_taps))
```

```python
import jax
import jax.numpy as jnp
from jax import lax
from jax.experimental import pallas as pl
from jax.experimental.pallas import tpu as pltpu
from jax.sharding import PartitionSpec as P

ITERS = 2
LANES = 128
GROUP = 8
VMEM_LIMIT = 48 * 1024 * 1024


def params():
    return pltpu.CompilerParams(vmem_limit_bytes=VMEM_LIMIT)


def in_vmem():
    return pl.BlockSpec(memory_space=pltpu.VMEM)


def in_smem():
    return pl.BlockSpec(memory_space=pltpu.SMEM)


def pack_kernel(place, following, own, strip, below, above, windows, rows, *, reach, blocks, row_blocks):
    chans, _, row_count, voxels = own.shape
    strip_rows = strip.shape[2]
    lane = lax.broadcasted_iota(jnp.int32, (1, LANES), 1)
    tall = lax.broadcasted_iota(jnp.int32, (strip_rows, voxels), 0)
    edge = LANES // 4
    block_rows = row_count // row_blocks
    window_rows = block_rows + 2 * reach
    for c in range(chans):
        rows[c, 0:reach, :] = below[c, 0, below.shape[2] - reach :, :]
        turned = pltpu.roll(below[c, 0, 0:strip_rows, :], place[1], 1)
        top = own[c, 0, 0:strip_rows, :]
        rows[c, reach : reach + strip_rows, :] = jnp.where(tall < place[0], 0.5 * (top + turned), top)
        rows[c, reach + strip_rows : reach + row_count, :] = own[c, 0, strip_rows:, :]
        turned = pltpu.roll(strip[c, 0], following[1], 1)
        top = above[c, 0, 0:strip_rows, :]
        after = jnp.where(tall < following[0], 0.5 * (top + turned), top)
        rows[c, reach + row_count : row_count + 2 * reach, :] = after[0:reach]
        whole = rows[c, 0 : row_count + 2 * reach, :]
        left, right = whole[:, :LANES], whole[:, LANES:]
        left_up, left_down = pltpu.roll(left, edge, 1), pltpu.roll(left, LANES - edge, 1)
        right_up, right_down = pltpu.roll(right, edge, 1), pltpu.roll(right, LANES - edge, 1)
        low, high = lane < edge, lane < LANES - edge
        cut = (
            jnp.where(low, 0.0, left_up),
            jnp.where(high, left_down, right_down),
            jnp.where(low, left_up, right_up),
            jnp.where(high, right_down, 0.0),
        )
        for b in range(row_blocks):
            for j in range(blocks):
                start = b * block_rows
                windows[(c * row_blocks + b) * blocks + j] = cut[j][start : start + window_rows]


def split(value):
    high = value.astype(jnp.bfloat16)
    low = (value - high.astype(jnp.float32)).astype(jnp.bfloat16)
    return high, low


def deconvolve_kernel(chan, axial, lateral, windows, result, bands, blurred, spread, estimate, *, reach, out_rows):
    planes, window_rows, _ = windows.shape
    axial_half, lateral_half = axial.shape[1] // 2, lateral.shape[1] // 2
    lateral_width = lateral.shape[1]
    c = chan[0]
    lateral_taps = [lateral[c, j] for j in range(lateral_width)]
    offset = lax.broadcasted_iota(jnp.int32, (LANES, LANES), 0) - lax.broadcasted_iota(jnp.int32, (LANES, LANES), 1)
    for which in range(2):
        band = jnp.zeros((LANES, LANES), jnp.float32)
        for j in range(lateral_width):
            tap = lateral_taps[j if which == 0 else lateral_width - 1 - j]
            band = jnp.where(offset == j - lateral_half, tap, band)
        high, low = split(band)
        bands[which, 0:LANES, 0:LANES] = high
        bands[which, 0:LANES, LANES:] = low
        bands[which, LANES:, 0:LANES] = high
        bands[which, LANES:, LANES:] = jnp.zeros_like(high)

    def along_x(value, which):
        both = jnp.concatenate(split(value), axis=1)
        product = jnp.dot(both, bands[which], preferred_element_type=jnp.float32)
        return product[:, :LANES] + product[:, LANES:]

    def along_y(source, q, g, flipped):
        total = None
        for j in range(lateral_width):
            tap = lateral_taps[lateral_width - 1 - j if flipped else j]
            term = tap * source[q, pl.ds(g * GROUP + j, GROUP), :]
            total = term if total is None else total + term
        return total

    def along_z(values, flipped):
        out = []
        for p in range(planes):
            total = None
            for q in range(planes):
                at = (p - q if flipped else q - p) + axial_half
                if 0 <= at < 2 * axial_half + 1:
                    term = axial[c, at] * values[q]
                    total = term if total is None else total + term
            out.append(total)
        return out

    def groups(rows):
        return -(-rows // GROUP)

    rows_left = window_rows
    origin = 0
    for sweep in range(ITERS):
        if sweep == 0:
            flat = windows[...].reshape(planes * window_rows, LANES)
            blurred[:, 0:window_rows, :] = along_x(flat, 0).reshape(planes, window_rows, LANES)
            blurred[:, window_rows:, :] = jnp.zeros((planes, blurred.shape[1] - window_rows, LANES), jnp.float32)
        else:
            tall = groups(rows_left) * GROUP
            flat = estimate[:, 0:tall, :].reshape(planes * tall, LANES)
            blurred[:, 0:tall, :] = along_x(flat, 0).reshape(planes, tall, LANES)
        rows_left -= 2 * lateral_half
        origin += lateral_half

        def forward(g, carry, origin=origin):
            mixed = along_z([along_y(blurred, q, g, False) for q in range(planes)], False)
            at = pl.ds(pl.multiple_of(g * GROUP, GROUP), GROUP)
            quotient = []
            for p in range(planes):
                joined = windows[p, pl.ds(g * GROUP + origin, GROUP), :]
                quotient.append(joined / jnp.where(joined > 0.0, mixed[p], 1.0))
            back = along_z(quotient, True)
            for p in range(planes):
                spread[p, at, :] = back[p]
            return carry

        forward_groups = groups(rows_left)
        last = (window_rows - origin) // GROUP
        lax.fori_loop(0, min(forward_groups, last), forward, 0)
        rows_left -= 2 * lateral_half
        origin += lateral_half

        def backward(g, carry):
            at = pl.ds(pl.multiple_of(g * GROUP, GROUP), GROUP)
            for q in range(planes):
                blurred[q, at, :] = along_y(spread, q, g, True)
            return carry

        tall = groups(rows_left) * GROUP
        lax.fori_loop(0, groups(rows_left), backward, 0)
        factor = along_x(blurred[:, 0:tall, :].reshape(planes * tall, LANES), 1).reshape(planes, tall, LANES)
        before = windows[:, origin : origin + tall, :] if sweep == 0 else estimate[:, lateral_half * 2 : lateral_half * 2 + tall, :]
        estimate[:, 0:tall, :] = before * factor
    half = out_rows // 2
    side = (LANES - LANES // 2) // 2
    lane = lax.broadcasted_iota(jnp.int32, (1, LANES), 1)
    for p in range(planes):
        first = pltpu.roll(estimate[p, 0:half, :], LANES - side, 1)
        second = pltpu.roll(estimate[p, half:out_rows, :], side, 1)
        result[p] = jnp.where(lane < LANES // 2, first, second)


def unpack_kernel(received, out, *, blocks, row_blocks):
    chans, _, row_count, voxels = out.shape
    half = received.shape[1]
    lane = lax.broadcasted_iota(jnp.int32, (1, LANES), 1)
    for c in range(chans):
        for b in range(row_blocks):
            for pair in range(blocks // 2):
                at = (c * row_blocks + b) * blocks + 2 * pair
                even, odd = received[at], received[at + 1]
                row = b * 2 * half
                columns = slice(pair * LANES, (pair + 1) * LANES)
                out[c, 0, row : row + half, columns] = jnp.where(lane < LANES // 2, even, pltpu.roll(odd, LANES // 2, 1))
                out[c, 0, row + half : row + 2 * half, columns] = jnp.where(lane < LANES // 2, pltpu.roll(even, LANES // 2, 1), odd)


def shards(observed, intersection_strip, axial_taps, lateral_taps, extents, section_skews):
    chans, _, row_count, voxels = observed.shape
    strip_rows = intersection_strip.shape[2]
    planes = lax.axis_size("plane")
    tiles = lax.axis_size("tile")
    lateral_half = lateral_taps.shape[1] // 2
    reach = 2 * ITERS * lateral_half
    blocks = voxels // (LANES // 2)
    row_blocks = planes // (chans * blocks)
    out_rows = row_count // row_blocks
    window_rows = out_rows + 2 * reach
    up = [(i, i + 1) for i in range(tiles - 1)]
    down = [(i + 1, i) for i in range(tiles - 1)]

    numbers = jnp.concatenate([extents, section_skews])
    marks = jnp.broadcast_to(numbers.astype(jnp.float32)[None, None, :, None], (chans, 1, 2, voxels))
    below = lax.ppermute(jnp.concatenate([intersection_strip, observed[:, :, row_count - strip_rows :]], axis=2), "tile", up)
    above = lax.ppermute(jnp.concatenate([observed[:, :, :strip_rows], marks], axis=2), "tile", down)
    following = above[0, 0, strip_rows:, 0].astype(jnp.int32)
    first_tile = lax.axis_index("tile") == 0
    place = jnp.where(jnp.stack([first_tile, False]), 0, numbers)

    windows = pl.pallas_call(
        lambda *refs: pack_kernel(*refs, reach=reach, blocks=blocks, row_blocks=row_blocks),
        out_shape=jax.ShapeDtypeStruct((planes, window_rows, LANES), jnp.float32),
        in_specs=[in_smem(), in_smem()] + [in_vmem()] * 4,
        out_specs=in_vmem(),
        scratch_shapes=[pltpu.VMEM((chans, row_count + 2 * reach, voxels), jnp.float32)],
        compiler_params=params(),
        name="pack",
    )(place, following, observed, intersection_strip, below, above)
    windows = lax.all_to_all(windows, "plane", 0, 0, tiled=True)

    channel = (lax.axis_index("plane") // (planes // chans)).astype(jnp.int32).reshape(1)
    padded = window_rows + 2 * GROUP
    result = pl.pallas_call(
        lambda *refs: deconvolve_kernel(*refs, reach=reach, out_rows=out_rows),
        out_shape=jax.ShapeDtypeStruct((planes, out_rows // 2, LANES), jnp.float32),
        in_specs=[in_smem()] * 3 + [in_vmem()],
        out_specs=in_vmem(),
        scratch_shapes=[
            pltpu.VMEM((2, 2 * LANES, 2 * LANES), jnp.bfloat16),
            pltpu.VMEM((planes, padded, LANES), jnp.float32),
            pltpu.VMEM((planes, padded, LANES), jnp.float32),
            pltpu.VMEM((planes, padded, LANES), jnp.float32),
        ],
        compiler_params=params(),
        name="deconvolve",
    )(channel, axial_taps, lateral_taps, windows)
    received = lax.all_to_all(result, "plane", 0, 0, tiled=True)
    return pl.pallas_call(
        lambda *refs: unpack_kernel(*refs, blocks=blocks, row_blocks=row_blocks),
        out_shape=jax.ShapeDtypeStruct(observed.shape, jnp.float32),
        in_specs=[in_vmem()],
        out_specs=in_vmem(),
        compiler_params=params(),
        name="unpack",
    )(received)


def solution(mesh):
    in_specs = (
        P(None, "plane", "tile", None),
        P(None, "plane", "tile", None),
        P(),
        P(),
        P("tile"),
        P("tile"),
    )
    out_specs = P(None, "plane", "tile", None)
    return jax.shard_map(shards, mesh=mesh, in_specs=in_specs, out_specs=out_specs, check_vma=False)
```

```python
import jax
import jax.numpy as jnp
from jax import lax
from jax.experimental import pallas as pl
from jax.experimental.pallas import tpu as pltpu
from jax.sharding import PartitionSpec as P

ITERS = 2
LANES = 128
GROUP = 8
VMEM_LIMIT = 48 * 1024 * 1024


def params():
    return pltpu.CompilerParams(vmem_limit_bytes=VMEM_LIMIT)


def in_vmem():
    return pl.BlockSpec(memory_space=pltpu.VMEM)


def in_smem():
    return pl.BlockSpec(memory_space=pltpu.SMEM)


def payload_kernel(facts, own, strip, to_core, to_chip):
    strip_rows = strip.shape[2]
    lower = facts[0] == 1
    numbers = jnp.where(
        lax.broadcasted_iota(jnp.int32, strip.shape, 3) < LANES,
        facts[1].astype(jnp.float32),
        facts[2].astype(jnp.float32),
    )
    up = (strip[...], own[:, :, own.shape[2] - strip_rows :, :])
    down = (own[:, :, :strip_rows, :], numbers)
    for k in range(2):
        at = slice(k * strip_rows, (k + 1) * strip_rows)
        to_core[:, :, at, :] = jnp.where(lower, down[k], up[k])
        to_chip[:, :, at, :] = jnp.where(lower, up[k], down[k])


def pack_kernel(facts, following, own, strip, core, chip, windows, rows, *, reach, blocks, row_blocks):
    chans, _, row_count, voxels = own.shape
    strip_rows = strip.shape[2]
    lane = lax.broadcasted_iota(jnp.int32, (1, LANES), 1)
    tall = lax.broadcasted_iota(jnp.int32, (strip_rows, voxels), 0)
    edge = LANES // 4
    block_rows = row_count // row_blocks
    window_rows = block_rows + 2 * reach
    lower = facts[0] == 1
    for c in range(chans):
        strip_before = jnp.where(lower, core[c, 0, :strip_rows, :], chip[c, 0, :strip_rows, :])
        rows_before = jnp.where(lower, core[c, 0, strip_rows:, :], chip[c, 0, strip_rows:, :])
        rows_after = jnp.where(lower, chip[c, 0, :strip_rows, :], core[c, 0, :strip_rows, :])
        rows[c, 0:reach, :] = rows_before[strip_rows - reach :]
        turned = pltpu.roll(strip_before, facts[2], 1)
        top = own[c, 0, 0:strip_rows, :]
        rows[c, reach : reach + strip_rows, :] = jnp.where(tall < facts[1], 0.5 * (top + turned), top)
        rows[c, reach + strip_rows : reach + row_count, :] = own[c, 0, strip_rows:, :]
        turned = pltpu.roll(strip[c, 0], following[1], 1)
        after = jnp.where(tall < following[0], 0.5 * (rows_after + turned), rows_after)
        rows[c, reach + row_count : row_count + 2 * reach, :] = after[0:reach]
        whole = rows[c, 0 : row_count + 2 * reach, :]
        left, right = whole[:, :LANES], whole[:, LANES:]
        left_up, left_down = pltpu.roll(left, edge, 1), pltpu.roll(left, LANES - edge, 1)
        right_up, right_down = pltpu.roll(right, edge, 1), pltpu.roll(right, LANES - edge, 1)
        low, high = lane < edge, lane < LANES - edge
        cut = (
            jnp.where(low, 0.0, left_up),
            jnp.where(high, left_down, right_down),
            jnp.where(low, left_up, right_up),
            jnp.where(high, right_down, 0.0),
        )
        for b in range(row_blocks):
            for j in range(blocks):
                start = b * block_rows
                windows[(c * row_blocks + b) * blocks + j] = cut[j][start : start + window_rows]


def split(value):
    high = value.astype(jnp.bfloat16)
    low = (value - high.astype(jnp.float32)).astype(jnp.bfloat16)
    return high, low


def deconvolve_kernel(chan, axial, lateral, windows, result, bands, blurred, spread, estimate, *, reach, out_rows):
    planes, window_rows, _ = windows.shape
    axial_half, lateral_half = axial.shape[1] // 2, lateral.shape[1] // 2
    lateral_width = lateral.shape[1]
    c = chan[0]
    lateral_taps = [lateral[c, j] for j in range(lateral_width)]
    offset = lax.broadcasted_iota(jnp.int32, (LANES, LANES), 0) - lax.broadcasted_iota(jnp.int32, (LANES, LANES), 1)
    for which in range(2):
        band = jnp.zeros((LANES, LANES), jnp.float32)
        for j in range(lateral_width):
            tap = lateral_taps[j if which == 0 else lateral_width - 1 - j]
            band = jnp.where(offset == j - lateral_half, tap, band)
        high, low = split(band)
        bands[which, 0:LANES, 0:LANES] = high
        bands[which, 0:LANES, LANES:] = low
        bands[which, LANES:, 0:LANES] = high
        bands[which, LANES:, LANES:] = jnp.zeros_like(high)

    def along_x(value, which):
        both = jnp.concatenate(split(value), axis=1)
        product = jnp.dot(both, bands[which], preferred_element_type=jnp.float32)
        return product[:, :LANES] + product[:, LANES:]

    def along_y(source, q, g, flipped):
        total = None
        for j in range(lateral_width):
            tap = lateral_taps[lateral_width - 1 - j if flipped else j]
            term = tap * source[q, pl.ds(g * GROUP + j, GROUP), :]
            total = term if total is None else total + term
        return total

    def along_z(values, flipped):
        out = []
        for p in range(planes):
            total = None
            for q in range(planes):
                at = (p - q if flipped else q - p) + axial_half
                if 0 <= at < 2 * axial_half + 1:
                    term = axial[c, at] * values[q]
                    total = term if total is None else total + term
            out.append(total)
        return out

    def groups(rows):
        return -(-rows // GROUP)

    rows_left = window_rows
    origin = 0
    for sweep in range(ITERS):
        if sweep == 0:
            flat = windows[...].reshape(planes * window_rows, LANES)
            blurred[:, 0:window_rows, :] = along_x(flat, 0).reshape(planes, window_rows, LANES)
            blurred[:, window_rows:, :] = jnp.zeros((planes, blurred.shape[1] - window_rows, LANES), jnp.float32)
        else:
            tall = groups(rows_left) * GROUP
            flat = estimate[:, 0:tall, :].reshape(planes * tall, LANES)
            blurred[:, 0:tall, :] = along_x(flat, 0).reshape(planes, tall, LANES)
        rows_left -= 2 * lateral_half
        origin += lateral_half

        def forward(g, carry, origin=origin):
            mixed = along_z([along_y(blurred, q, g, False) for q in range(planes)], False)
            at = pl.ds(pl.multiple_of(g * GROUP, GROUP), GROUP)
            quotient = []
            for p in range(planes):
                joined = windows[p, pl.ds(g * GROUP + origin, GROUP), :]
                quotient.append(joined / jnp.where(joined > 0.0, mixed[p], 1.0))
            back = along_z(quotient, True)
            for p in range(planes):
                spread[p, at, :] = back[p]
            return carry

        forward_groups = groups(rows_left)
        last = (window_rows - origin) // GROUP
        lax.fori_loop(0, min(forward_groups, last), forward, 0)
        rows_left -= 2 * lateral_half
        origin += lateral_half

        def backward(g, carry):
            at = pl.ds(pl.multiple_of(g * GROUP, GROUP), GROUP)
            for q in range(planes):
                blurred[q, at, :] = along_y(spread, q, g, True)
            return carry

        tall = groups(rows_left) * GROUP
        lax.fori_loop(0, groups(rows_left), backward, 0)
        factor = along_x(blurred[:, 0:tall, :].reshape(planes * tall, LANES), 1).reshape(planes, tall, LANES)
        before = windows[:, origin : origin + tall, :] if sweep == 0 else estimate[:, lateral_half * 2 : lateral_half * 2 + tall, :]
        estimate[:, 0:tall, :] = before * factor
    half = out_rows // 2
    side = (LANES - LANES // 2) // 2
    lane = lax.broadcasted_iota(jnp.int32, (1, LANES), 1)
    for p in range(planes):
        first = pltpu.roll(estimate[p, 0:half, :], LANES - side, 1)
        second = pltpu.roll(estimate[p, half:out_rows, :], side, 1)
        result[p] = jnp.where(lane < LANES // 2, first, second)


def unpack_kernel(received, out, *, blocks, row_blocks):
    chans, _, row_count, voxels = out.shape
    half = received.shape[1]
    lane = lax.broadcasted_iota(jnp.int32, (1, LANES), 1)
    for c in range(chans):
        for b in range(row_blocks):
            for pair in range(blocks // 2):
                at = (c * row_blocks + b) * blocks + 2 * pair
                even, odd = received[at], received[at + 1]
                row = b * 2 * half
                columns = slice(pair * LANES, (pair + 1) * LANES)
                out[c, 0, row : row + half, columns] = jnp.where(lane < LANES // 2, even, pltpu.roll(odd, LANES // 2, 1))
                out[c, 0, row + half : row + 2 * half, columns] = jnp.where(lane < LANES // 2, pltpu.roll(even, LANES // 2, 1), odd)


def shards(observed, intersection_strip, axial_taps, lateral_taps, extents, section_skews):
    chans, _, row_count, voxels = observed.shape
    strip_rows = intersection_strip.shape[2]
    planes = lax.axis_size("plane")
    tiles = lax.axis_size("tile")
    lateral_half = lateral_taps.shape[1] // 2
    reach = 2 * ITERS * lateral_half
    blocks = voxels // (LANES // 2)
    row_blocks = planes // (chans * blocks)
    out_rows = row_count // row_blocks
    window_rows = out_rows + 2 * reach
    cores = [(i, i ^ 1) for i in range(tiles)]
    chips = [pair for i in range(1, tiles - 1, 2) for pair in ((i, i + 1), (i + 1, i))]

    tile = lax.axis_index("tile")
    facts = jnp.stack([tile % 2, jnp.where(tile == 0, 0, extents[0]), section_skews[0]]).astype(jnp.int32)
    payload = jax.ShapeDtypeStruct((chans, 1, 2 * strip_rows, voxels), jnp.float32)
    to_core, to_chip = pl.pallas_call(
        payload_kernel,
        out_shape=(payload, payload),
        in_specs=[in_smem(), in_vmem(), in_vmem()],
        out_specs=(in_vmem(), in_vmem()),
        compiler_params=params(),
        name="payload",
    )(facts, observed, intersection_strip)
    core = lax.ppermute(to_core, "tile", cores)
    chip = lax.ppermute(to_chip, "tile", chips)
    marks = jnp.where(tile % 2 == 0, core[0, 0, strip_rows, ::LANES], chip[0, 0, strip_rows, ::LANES])
    following = marks.astype(jnp.int32)

    windows = pl.pallas_call(
        lambda *refs: pack_kernel(*refs, reach=reach, blocks=blocks, row_blocks=row_blocks),
        out_shape=jax.ShapeDtypeStruct((planes, window_rows, LANES), jnp.float32),
        in_specs=[in_smem(), in_smem()] + [in_vmem()] * 4,
        out_specs=in_vmem(),
        scratch_shapes=[pltpu.VMEM((chans, row_count + 2 * reach, voxels), jnp.float32)],
        compiler_params=params(),
        name="pack",
    )(facts, following, observed, intersection_strip, core, chip)
    windows = lax.all_to_all(windows, "plane", 0, 0, tiled=True)

    channel = (lax.axis_index("plane") // (planes // chans)).astype(jnp.int32).reshape(1)
    padded = window_rows + 2 * GROUP
    result = pl.pallas_call(
        lambda *refs: deconvolve_kernel(*refs, reach=reach, out_rows=out_rows),
        out_shape=jax.ShapeDtypeStruct((planes, out_rows // 2, LANES), jnp.float32),
        in_specs=[in_smem()] * 3 + [in_vmem()],
        out_specs=in_vmem(),
        scratch_shapes=[
            pltpu.VMEM((2, 2 * LANES, 2 * LANES), jnp.bfloat16),
            pltpu.VMEM((planes, padded, LANES), jnp.float32),
            pltpu.VMEM((planes, padded, LANES), jnp.float32),
            pltpu.VMEM((planes, padded, LANES), jnp.float32),
        ],
        compiler_params=params(),
        name="deconvolve",
    )(channel, axial_taps, lateral_taps, windows)
    received = lax.all_to_all(result, "plane", 0, 0, tiled=True)
    return pl.pallas_call(
        lambda *refs: unpack_kernel(*refs, blocks=blocks, row_blocks=row_blocks),
        out_shape=jax.ShapeDtypeStruct(observed.shape, jnp.float32),
        in_specs=[in_vmem()],
        out_specs=in_vmem(),
        compiler_params=params(),
        name="unpack",
    )(received)


def solution(mesh):
    in_specs = (
        P(None, "plane", "tile", None),
        P(None, "plane", "tile", None),
        P(),
        P(),
        P("tile"),
        P("tile"),
    )
    out_specs = P(None, "plane", "tile", None)
    return jax.shard_map(shards, mesh=mesh, in_specs=in_specs, out_specs=out_specs, check_vma=False)
```

```python
import jax
import jax.numpy as jnp
from jax import lax
from jax.experimental import pallas as pl
from jax.experimental.pallas import tpu as pltpu
from jax.sharding import PartitionSpec as P

ITERS = 2
LANES = 128
GROUP = 8
VMEM_LIMIT = 48 * 1024 * 1024


def params():
    return pltpu.CompilerParams(vmem_limit_bytes=VMEM_LIMIT)


def in_vmem():
    return pl.BlockSpec(memory_space=pltpu.VMEM)


def in_smem():
    return pl.BlockSpec(memory_space=pltpu.SMEM)


def payload_kernel(facts, own, strip, to_core, to_chip, sems):
    strip_rows = strip.shape[2]
    low, high = slice(0, strip_rows), slice(strip_rows, 2 * strip_rows)

    def fill(up, down):
        copies = []
        for c in range(strip.shape[0]):
            pieces = (
                (strip.at[c], up.at[c, :, low, :]),
                (own.at[c, :, own.shape[2] - strip_rows :, :], up.at[c, :, high, :]),
                (own.at[c, :, low, :], down.at[c, :, low, :]),
            )
            for source, target in pieces:
                copies.append(pltpu.make_async_copy(source, target, sems.at[len(copies)]))
        for copy in copies:
            copy.start()
        column = lax.broadcasted_iota(jnp.int32, strip.shape, 3)
        down[:, :, high, :] = jnp.where(column < LANES, facts[1], facts[2]).astype(jnp.float32)
        for copy in copies:
            copy.wait()

    @pl.when(facts[0] == 1)
    def _():
        fill(to_chip, to_core)

    @pl.when(facts[0] == 0)
    def _():
        fill(to_core, to_chip)


def pack_kernel(facts, to_core, to_chip, core, chip, windows, rows, *, reach, blocks, row_blocks):
    chans, _, row_count, voxels = core.shape
    strip_rows = row_count // 2
    lane = lax.broadcasted_iota(jnp.int32, (1, LANES), 1)
    tall = lax.broadcasted_iota(jnp.int32, (strip_rows, voxels), 0)
    edge = LANES // 4
    block_rows = row_count // row_blocks
    window_rows = block_rows + 2 * reach
    lower = facts[0] == 1

    def pick(low, high, c, part):
        at = slice(part * strip_rows, (part + 1) * strip_rows)
        return jnp.where(lower, low[c, 0, at, :], high[c, 0, at, :])

    numbers = pick(chip, core, 0, 1)[0:GROUP].astype(jnp.int32)
    next_extent, next_skew = jnp.max(numbers[:, :LANES]), jnp.max(numbers[:, LANES:])
    for c in range(chans):
        rows[c, 0:reach, :] = pick(core, chip, c, 1)[strip_rows - reach :]
        turned = pltpu.roll(pick(core, chip, c, 0), facts[2], 1)
        top = pick(to_core, to_chip, c, 0)
        rows[c, reach : reach + strip_rows, :] = jnp.where(tall < facts[1], 0.5 * (top + turned), top)
        rows[c, reach + strip_rows : reach + row_count, :] = pick(to_chip, to_core, c, 1)
        turned = pltpu.roll(pick(to_chip, to_core, c, 0), next_skew, 1)
        top = pick(chip, core, c, 0)
        after = jnp.where(tall < next_extent, 0.5 * (top + turned), top)
        rows[c, reach + row_count : row_count + 2 * reach, :] = after[0:reach]
        whole = rows[c, 0 : row_count + 2 * reach, :]
        left, right = whole[:, :LANES], whole[:, LANES:]
        left_up, left_down = pltpu.roll(left, edge, 1), pltpu.roll(left, LANES - edge, 1)
        right_up, right_down = pltpu.roll(right, edge, 1), pltpu.roll(right, LANES - edge, 1)
        low, high = lane < edge, lane < LANES - edge
        cut = (
            jnp.where(low, 0.0, left_up),
            jnp.where(high, left_down, right_down),
            jnp.where(low, left_up, right_up),
            jnp.where(high, right_down, 0.0),
        )
        for b in range(row_blocks):
            for j in range(blocks):
                start = b * block_rows
                windows[(c * row_blocks + b) * blocks + j] = cut[j][start : start + window_rows]


def split(value):
    high = value.astype(jnp.bfloat16)
    low = (value - high.astype(jnp.float32)).astype(jnp.bfloat16)
    return high, low


def stages(window_rows, lateral_half):
    def tiled(rows):
        return -(-rows // 16) * 16

    return [
        (tiled(window_rows - 2 * k * lateral_half), tiled(window_rows - 2 * (k + 1) * lateral_half))
        for k in range(2 * ITERS)
    ]


def bands_kernel(chan, axial, lateral, along_z, along_x, *along_y, spans):
    width = lateral.shape[1]
    taps = [lateral[chan[0], j] for j in range(width)]
    for j in range(axial.shape[1]):
        along_z[j] = jnp.full((GROUP, LANES), axial[chan[0], j], jnp.float32)
    offset = lax.broadcasted_iota(jnp.int32, (LANES, LANES), 0) - lax.broadcasted_iota(jnp.int32, (LANES, LANES), 1)

    def band(order, where, first):
        total = jnp.zeros((LANES, LANES), jnp.float32)
        for j in range(width):
            total = jnp.where(where == j + first, order[j], total)
        return split(total)

    for which in range(2):
        order = taps if which == 0 else taps[::-1]
        high, low = band(order, offset, -(width // 2))
        along_x[which, :LANES, :LANES] = high
        along_x[which, :LANES, LANES:] = low
        along_x[which, LANES:, :LANES] = high
        along_x[which, LANES:, LANES:] = jnp.zeros_like(low)
        high, low = band(order, -offset, 0)
        for k in range(which, len(spans), 2):
            read, written = spans[k]
            top, bottom = high[:written, :read], low[:written, :read]
            along_y[k][:written] = jnp.concatenate([top, top], axis=1)
            along_y[k][written:] = jnp.concatenate([bottom, jnp.zeros_like(bottom)], axis=1)


def deconvolve_kernel(windows, axial, x_bands, *refs, spans, lateral_half, out_rows):
    y_bands, (result, blurred, estimate) = refs[: len(spans)], refs[len(spans) :]
    planes, window_rows, _ = windows.shape
    axial_half = axial.shape[0] // 2
    columns = [slice(q * LANES, (q + 1) * LANES) for q in range(planes)]

    def along_x(values, which):
        out = []
        for q in range(0, planes, 2):
            pair = jnp.concatenate(values[q : q + 2], axis=0)
            product = jnp.dot(jnp.concatenate(split(pair), axis=1), x_bands[which], preferred_element_type=jnp.float32)
            product = product[:, :LANES] + product[:, LANES:]
            out += [product[: pair.shape[0] // 2], product[pair.shape[0] // 2 :]]
        return out

    def along_y(k):
        read, written = spans[k]
        for q in range(0, planes, 2):
            pair = slice(q * LANES, (q + 2) * LANES)
            both = jnp.concatenate(split(blurred[0:read, pair]), axis=0)
            product = jnp.dot(y_bands[k][...], both, preferred_element_type=jnp.float32)
            blurred[0:written, pair] = product[:written] + product[written:]

    def along_z(values, flipped):
        out = []
        for p in range(planes):
            total = None
            for q in range(planes):
                at = (p - q if flipped else q - p) + axial_half
                if 0 <= at < 2 * axial_half + 1:
                    term = axial[at] * values[q]
                    total = term if total is None else total + term
            out.append(total)
        return out

    origin = 0
    for sweep in range(ITERS):
        read, written = spans[2 * sweep]
        if sweep == 0:
            values = along_x([windows[p] for p in range(planes)], 0)
            blurred[window_rows:read, :] = jnp.zeros((read - window_rows, planes * LANES), jnp.float32)
        else:
            values = along_x([estimate[0:read, columns[p]] for p in range(planes)], 0)
        for p in range(planes):
            blurred[0 : values[p].shape[0], columns[p]] = values[p]
        along_y(2 * sweep)
        origin += lateral_half
        for row in range(0, written, GROUP):
            at = slice(row, row + GROUP)
            mixed = along_z([blurred[at, columns[q]] for q in range(planes)], False)
            quotient = []
            for p in range(planes):
                joined = windows[p, row + origin : row + origin + GROUP, :]
                quotient.append(joined / jnp.where(joined > 0.0, mixed[p], 1.0))
            back = along_z(quotient, True)
            for p in range(planes):
                blurred[at, columns[p]] = back[p]
        read, written = spans[2 * sweep + 1]
        along_y(2 * sweep + 1)
        origin += lateral_half
        factor = along_x([blurred[0:written, columns[p]] for p in range(planes)], 1)
        for p in range(planes):
            if sweep == 0:
                before = windows[p, origin : origin + written, :]
            else:
                before = estimate[2 * lateral_half : 2 * lateral_half + written, columns[p]]
            estimate[0:written, columns[p]] = before * factor[p]
    half = out_rows // 2
    side = (LANES - LANES // 2) // 2
    lane = lax.broadcasted_iota(jnp.int32, (1, LANES), 1)
    for p in range(planes):
        first = pltpu.roll(estimate[0:half, columns[p]], LANES - side, 1)
        second = pltpu.roll(estimate[half:out_rows, columns[p]], side, 1)
        result[p] = jnp.where(lane < LANES // 2, first, second)


def unpack_kernel(received, out, *, blocks, row_blocks):
    chans, _, row_count, voxels = out.shape
    half = received.shape[1]
    lane = lax.broadcasted_iota(jnp.int32, (1, LANES), 1)
    for c in range(chans):
        for b in range(row_blocks):
            for pair in range(blocks // 2):
                at = (c * row_blocks + b) * blocks + 2 * pair
                even, odd = received[at], received[at + 1]
                row = b * 2 * half
                columns = slice(pair * LANES, (pair + 1) * LANES)
                out[c, 0, row : row + half, columns] = jnp.where(lane < LANES // 2, even, pltpu.roll(odd, LANES // 2, 1))
                out[c, 0, row + half : row + 2 * half, columns] = jnp.where(lane < LANES // 2, pltpu.roll(even, LANES // 2, 1), odd)


def shards(observed, intersection_strip, axial_taps, lateral_taps, extents, section_skews):
    chans, _, row_count, voxels = observed.shape
    strip_rows = intersection_strip.shape[2]
    planes = lax.axis_size("plane")
    tiles = lax.axis_size("tile")
    lateral_half = lateral_taps.shape[1] // 2
    reach = 2 * ITERS * lateral_half
    blocks = voxels // (LANES // 2)
    row_blocks = planes // (chans * blocks)
    out_rows = row_count // row_blocks
    window_rows = out_rows + 2 * reach
    cores = [(i, i ^ 1) for i in range(tiles)]
    chips = [pair for i in range(1, tiles - 1, 2) for pair in ((i, i + 1), (i + 1, i))]

    tile = lax.axis_index("tile")
    facts = jnp.stack([tile % 2, jnp.where(tile == 0, 0, extents[0]), section_skews[0]]).astype(jnp.int32)
    payload = jax.ShapeDtypeStruct((chans, 1, 2 * strip_rows, voxels), jnp.float32)
    to_core, to_chip = pl.pallas_call(
        payload_kernel,
        out_shape=(payload, payload),
        in_specs=[in_smem(), pl.BlockSpec(memory_space=pltpu.HBM), pl.BlockSpec(memory_space=pltpu.HBM)],
        out_specs=(in_vmem(), in_vmem()),
        scratch_shapes=[pltpu.SemaphoreType.DMA((3 * chans,))],
        compiler_params=params(),
        name="payload",
    )(facts, pltpu.with_memory_space_constraint(observed, pltpu.HBM), pltpu.with_memory_space_constraint(intersection_strip, pltpu.HBM))
    chip = lax.ppermute(to_chip, "tile", chips)
    core = lax.ppermute(to_core, "tile", cores)
    windows = pl.pallas_call(
        lambda *refs: pack_kernel(*refs, reach=reach, blocks=blocks, row_blocks=row_blocks),
        out_shape=jax.ShapeDtypeStruct((planes, window_rows, LANES), jnp.float32),
        in_specs=[in_smem()] + [in_vmem()] * 4,
        out_specs=in_vmem(),
        scratch_shapes=[pltpu.VMEM((chans, row_count + 2 * reach, voxels), jnp.float32)],
        compiler_params=params(),
        name="pack",
    )(facts, to_core, to_chip, core, chip)
    windows = lax.all_to_all(windows, "plane", 0, 0, tiled=True)

    channel = (lax.axis_index("plane") // (planes // chans)).astype(jnp.int32).reshape(1)
    spans = stages(window_rows, lateral_half)
    bands = pl.pallas_call(
        lambda *refs: bands_kernel(*refs, spans=spans),
        out_shape=[
            jax.ShapeDtypeStruct((axial_taps.shape[1], GROUP, LANES), jnp.float32),
            jax.ShapeDtypeStruct((2, 2 * LANES, 2 * LANES), jnp.bfloat16),
        ]
        + [jax.ShapeDtypeStruct((2 * written, 2 * read), jnp.bfloat16) for read, written in spans],
        in_specs=[in_smem()] * 3,
        out_specs=[in_vmem()] * (2 + len(spans)),
        cost_estimate=pl.CostEstimate(flops=1 << 20, bytes_accessed=1 << 20, transcendentals=0),
        compiler_params=params(),
        name="bands",
    )(channel, axial_taps, lateral_taps)
    result = pl.pallas_call(
        lambda *refs: deconvolve_kernel(*refs, spans=spans, lateral_half=lateral_half, out_rows=out_rows),
        out_shape=jax.ShapeDtypeStruct((planes, out_rows // 2, LANES), jnp.float32),
        in_specs=[in_vmem()] * (3 + len(spans)),
        out_specs=in_vmem(),
        scratch_shapes=[
            pltpu.VMEM((spans[0][0], planes * LANES), jnp.float32),
            pltpu.VMEM((spans[1][1], planes * LANES), jnp.float32),
        ],
        compiler_params=params(),
        name="deconvolve",
    )(windows, *bands)
    received = lax.all_to_all(result, "plane", 0, 0, tiled=True)
    return pl.pallas_call(
        lambda *refs: unpack_kernel(*refs, blocks=blocks, row_blocks=row_blocks),
        out_shape=jax.ShapeDtypeStruct(observed.shape, jnp.float32),
        in_specs=[in_vmem()],
        out_specs=in_vmem(),
        compiler_params=params(),
        name="unpack",
    )(received)


def solution(mesh):
    in_specs = (
        P(None, "plane", "tile", None),
        P(None, "plane", "tile", None),
        P(),
        P(),
        P("tile"),
        P("tile"),
    )
    out_specs = P(None, "plane", "tile", None)
    return jax.shard_map(shards, mesh=mesh, in_specs=in_specs, out_specs=out_specs, check_vma=False)
```

```python
import jax
import jax.numpy as jnp
from jax import lax
from jax.experimental import pallas as pl
from jax.experimental.pallas import tpu as pltpu
from jax.sharding import PartitionSpec as P

ITERS = 2
LANES = 128
GROUP = 8
VMEM_LIMIT = 48 * 1024 * 1024


def params():
    return pltpu.CompilerParams(vmem_limit_bytes=VMEM_LIMIT)


def in_vmem():
    return pl.BlockSpec(memory_space=pltpu.VMEM)


def in_smem():
    return pl.BlockSpec(memory_space=pltpu.SMEM)


def split(value):
    high = value.astype(jnp.bfloat16)
    low = (value - high.astype(jnp.float32)).astype(jnp.bfloat16)
    return high, low


def payload_kernel(own, strip, extents, skews, to_core, to_chip, sems):
    strip_rows = strip.shape[2]
    tile = lax.axis_index("tile")
    low, high = slice(0, strip_rows), slice(strip_rows, 2 * strip_rows)

    def fill(up, down):
        pieces = []
        for c in range(strip.shape[0]):
            pieces += [
                (strip.at[c], up.at[c, :, low, :]),
                (own.at[c, :, own.shape[2] - strip_rows :, :], up.at[c, :, high, :]),
                (own.at[c, :, low, :], down.at[c, :, low, :]),
            ]
        copies = [pltpu.make_async_copy(source, target, sems.at[i]) for i, (source, target) in enumerate(pieces)]
        for copy in copies:
            copy.start()
        extent = jnp.where(tile == 0, 0, extents[0])
        column = lax.broadcasted_iota(jnp.int32, strip.shape, 3)
        down[:, :, high, :] = jnp.where(column < LANES, extent, skews[0]).astype(jnp.float32)
        for copy in copies:
            copy.wait()

    @pl.when(tile % 2 == 1)
    def _():
        fill(to_chip, to_core)

    @pl.when(tile % 2 == 0)
    def _():
        fill(to_core, to_chip)


def pack_kernel(to_core, to_chip, core, chip, _, windows, *, blocks):
    chans, _, row_count, voxels = core.shape
    half = row_count // 2
    block = voxels // blocks
    lane = lax.broadcasted_iota(jnp.int32, (1, LANES), 1)
    tall = lax.broadcasted_iota(jnp.int32, (half, voxels), 0)
    lower = lax.axis_index("tile") % 2 == 1

    def pick(low, high, c, part):
        at = slice(part * half, (part + 1) * half)
        return jnp.where(lower, low[c, 0, at, :], high[c, 0, at, :])

    def numbers(low, high):
        both = pick(low, high, 0, 1)[0:GROUP].astype(jnp.int32)
        return jnp.max(both[:, :LANES]), jnp.max(both[:, LANES:])

    extent, skew = numbers(to_core, to_chip)
    next_extent, next_skew = numbers(chip, core)
    for c in range(chans):
        turned = pltpu.roll(pick(core, chip, c, 0), skew, 1)
        top = pick(to_core, to_chip, c, 0)
        top = jnp.where(tall < extent, 0.5 * (top + turned), top)
        bottom = pick(to_chip, to_core, c, 1)
        turned = pltpu.roll(pick(to_chip, to_core, c, 0), next_skew, 1)
        after = chip[c, 0, :half, :]
        after = jnp.where(tall < next_extent, 0.5 * (after + turned), after)
        before = chip[c, 0, half:, :]
        rows = [jnp.where(lower, top, bottom), jnp.where(lower, bottom, top), jnp.where(lower, after, before)]
        rows = jnp.concatenate(rows, axis=0)
        for j in range(blocks):
            start = j * block - (LANES - LANES // 2) // 2
            window = pltpu.roll(rows, -start % voxels, 1)[:, :LANES]
            inside = (lane >= -start) & (lane < voxels - start)
            windows[c * blocks + j] = jnp.where(inside, window, 0.0)


def stages(window_rows, lateral_half, skipped):
    def tiled(rows):
        return -(-rows // 16) * 16

    counts = [window_rows] + [window_rows - 2 * skipped - 2 * k * lateral_half for k in range(1, 2 * ITERS + 1)]
    return [(tiled(read), tiled(written)) for read, written in zip(counts[:-1], counts[1:])]


def bands_kernel(axial, lateral, along_z, along_x, *along_y, spans, skipped, blocks):
    width = lateral.shape[1]
    chan = lax.axis_index("plane") // blocks
    taps = [lateral[chan, j] for j in range(width)]
    for j in range(axial.shape[1]):
        along_z[j] = jnp.full((GROUP, LANES), axial[chan, j], jnp.float32)
    offset = lax.broadcasted_iota(jnp.int32, (LANES, LANES), 0) - lax.broadcasted_iota(jnp.int32, (LANES, LANES), 1)

    def band(order, where, first):
        total = jnp.zeros((LANES, LANES), jnp.float32)
        for j in range(width):
            total = jnp.where(where == j + first, order[j], total)
        return split(total)

    for which in range(2):
        order = taps if which == 0 else taps[::-1]
        high, low = band(order, offset, -(width // 2))
        along_x[which, :LANES, :LANES] = high
        along_x[which, :LANES, LANES:] = low
        along_x[which, LANES:, :LANES] = high
        along_x[which, LANES:, LANES:] = jnp.zeros_like(low)
        for k in range(which, len(spans), 2):
            read, written = spans[k]
            high, low = band(order, -offset, skipped if k == 0 else 0)
            top, bottom = high[:written, :read], low[:written, :read]
            along_y[k][:written] = jnp.concatenate([top, top], axis=1)
            along_y[k][written:] = jnp.concatenate([bottom, jnp.zeros_like(bottom)], axis=1)


def deconvolve_kernel(own, core, axial, x_bands, *refs, spans, lateral_half, skipped, blocks):
    y_bands, (result, windows, blurred, estimate) = refs[: len(spans)], refs[len(spans) :]
    planes, window_rows, _ = windows.shape
    half = core.shape[1]
    out_rows = 2 * half
    axial_half = axial.shape[0] // 2
    columns = [slice(q * LANES, (q + 1) * LANES) for q in range(planes)]
    lower = lax.axis_index("tile") % 2 == 1
    for place, piece in enumerate((core[...], *(own[:, i * half : (i + 1) * half, :] for i in range(3)))):
        at = jnp.where(lower, place, 3 - place) * half
        windows[:, pl.ds(pl.multiple_of(at, half), half), :] = piece

    def along_x(values, which):
        out = []
        for q in range(0, planes, 2):
            pair = jnp.concatenate(values[q : q + 2], axis=0)
            product = jnp.dot(jnp.concatenate(split(pair), axis=1), x_bands[which], preferred_element_type=jnp.float32)
            product = product[:, :LANES] + product[:, LANES:]
            out += [product[: pair.shape[0] // 2], product[pair.shape[0] // 2 :]]
        return out

    def along_y(k):
        read, written = spans[k]
        for q in range(0, planes, 2):
            pair = slice(q * LANES, (q + 2) * LANES)
            both = jnp.concatenate(split(blurred[0:read, pair]), axis=0)
            product = jnp.dot(y_bands[k][...], both, preferred_element_type=jnp.float32)
            blurred[0:written, pair] = product[:written] + product[written:]

    def along_z(values, flipped):
        out = []
        for p in range(planes):
            total = None
            for q in range(planes):
                at = (p - q if flipped else q - p) + axial_half
                if 0 <= at < 2 * axial_half + 1:
                    term = axial[at] * values[q]
                    total = term if total is None else total + term
            out.append(total)
        return out

    origin = skipped
    for sweep in range(ITERS):
        read, written = spans[2 * sweep]
        source = [windows[p] if sweep == 0 else estimate[0:read, columns[p]] for p in range(planes)]
        for p, value in enumerate(along_x(source, 0)):
            blurred[0:read, columns[p]] = value
        along_y(2 * sweep)
        origin += lateral_half
        for row in range(0, written, GROUP):
            at = slice(row, row + GROUP)
            mixed = along_z([blurred[at, columns[q]] for q in range(planes)], False)
            quotient = []
            for p in range(planes):
                joined = windows[p, row + origin : row + origin + GROUP, :]
                quotient.append(joined / jnp.where(joined > 0.0, mixed[p], 1.0))
            back = along_z(quotient, True)
            for p in range(planes):
                blurred[at, columns[p]] = back[p]
        read, written = spans[2 * sweep + 1]
        along_y(2 * sweep + 1)
        origin += lateral_half
        factor = along_x([blurred[0:written, columns[p]] for p in range(planes)], 1)
        for p in range(planes):
            if sweep == 0:
                before = windows[p, origin : origin + written, :]
            else:
                before = estimate[2 * lateral_half : 2 * lateral_half + written, columns[p]]
            estimate[0:written, columns[p]] = before * factor[p]
    voxels = 2 * LANES // blocks
    parts = LANES // voxels
    tall = out_rows // parts
    side = (LANES - LANES // 2) // 2
    lane = lax.broadcasted_iota(jnp.int32, (1, LANES), 1)
    for p in range(planes):
        packed = None
        for m in range(parts):
            piece = pltpu.roll(estimate[m * tall : (m + 1) * tall, columns[p]], (m * voxels - side) % LANES, 1)
            packed = piece if packed is None else jnp.where(lane < m * voxels, packed, piece)
        result[p] = packed


def unpack_kernel(received, out, *, blocks):
    chans, _, row_count, voxels = out.shape
    block = voxels // blocks
    parts = LANES // block
    tall = row_count // parts
    lane = lax.broadcasted_iota(jnp.int32, (1, LANES), 1)
    for c in range(chans):
        for column in range(0, voxels, LANES):
            first = c * blocks + column // block
            for m in range(parts):
                whole = None
                for i in range(parts):
                    value = received[first + i]
                    piece = value if i == m else pltpu.roll(value, (i - m) * block % LANES, 1)
                    whole = piece if whole is None else jnp.where(lane < i * block, whole, piece)
                out[c, 0, m * tall : (m + 1) * tall, column : column + LANES] = whole


def shards(observed, intersection_strip, axial_taps, lateral_taps, extents, section_skews):
    chans, _, row_count, voxels = observed.shape
    planes = lax.axis_size("plane")
    tiles = lax.axis_size("tile")
    half = row_count // 2
    blocks = planes // chans
    lateral_half = lateral_taps.shape[1] // 2
    skipped = half - 2 * ITERS * lateral_half
    window_rows = row_count + 2 * half
    cores = [(i, i ^ 1) for i in range(tiles)]
    chips = [pair for i in range(1, tiles - 1, 2) for pair in ((i, i + 1), (i + 1, i))]

    payload = jax.ShapeDtypeStruct((chans, 1, 2 * half, voxels), jnp.float32)
    to_core, to_chip = pl.pallas_call(
        payload_kernel,
        out_shape=(payload, payload),
        in_specs=[pl.BlockSpec(memory_space=pltpu.HBM)] * 2 + [in_smem()] * 2,
        out_specs=(in_vmem(), in_vmem()),
        scratch_shapes=[pltpu.SemaphoreType.DMA((3 * chans,))],
        compiler_params=params(),
        name="payload",
    )(*(pltpu.with_memory_space_constraint(array, pltpu.HBM) for array in (observed, intersection_strip)), extents, section_skews)
    chip = lax.ppermute(to_chip, "tile", chips)
    core = lax.ppermute(to_core, "tile", cores)
    spans = stages(window_rows, lateral_half, skipped)
    bands = pl.pallas_call(
        lambda *refs: bands_kernel(*refs, spans=spans, skipped=skipped, blocks=blocks),
        out_shape=[
            jax.ShapeDtypeStruct((axial_taps.shape[1], GROUP, LANES), jnp.float32),
            jax.ShapeDtypeStruct((2, 2 * LANES, 2 * LANES), jnp.bfloat16),
        ]
        + [jax.ShapeDtypeStruct((2 * written, 2 * read), jnp.bfloat16) for read, written in spans],
        in_specs=[in_smem()] * 2,
        out_specs=[in_vmem()] * (2 + len(spans)),
        cost_estimate=pl.CostEstimate(flops=1 << 20, bytes_accessed=1 << 20, transcendentals=0),
        compiler_params=params(),
        name="bands",
    )(axial_taps, lateral_taps)
    windows = pl.pallas_call(
        lambda *refs: pack_kernel(*refs, blocks=blocks),
        out_shape=jax.ShapeDtypeStruct((planes, row_count + half, LANES), jnp.float32),
        in_specs=[in_vmem()] * 4 + [pl.BlockSpec(memory_space=pl.ANY)],
        out_specs=in_vmem(),
        compiler_params=params(),
        name="pack",
    )(to_core, to_chip, core, chip, bands[0])
    windows = lax.all_to_all(windows, "plane", 0, 0, tiled=True)

    across = lax.ppermute(windows[:, :half, :], "tile", cores)
    result = pl.pallas_call(
        lambda *refs: deconvolve_kernel(
            *refs, spans=spans, lateral_half=lateral_half, skipped=skipped, blocks=blocks
        ),
        out_shape=jax.ShapeDtypeStruct((planes, row_count * voxels // blocks // LANES, LANES), jnp.float32),
        in_specs=[in_vmem()] * (4 + len(spans)),
        out_specs=in_vmem(),
        scratch_shapes=[
            pltpu.VMEM((planes, window_rows, LANES), jnp.float32),
            pltpu.VMEM((spans[0][0], planes * LANES), jnp.float32),
            pltpu.VMEM((spans[1][1], planes * LANES), jnp.float32),
        ],
        compiler_params=params(),
        name="deconvolve",
    )(windows, across, *bands)
    received = lax.all_to_all(result, "plane", 0, 0, tiled=True)
    return pl.pallas_call(
        lambda *refs: unpack_kernel(*refs, blocks=blocks),
        out_shape=jax.ShapeDtypeStruct(observed.shape, jnp.float32),
        in_specs=[in_vmem()],
        out_specs=in_vmem(),
        compiler_params=params(),
        name="unpack",
    )(received)


def solution(mesh):
    in_specs = (
        P(None, "plane", "tile", None),
        P(None, "plane", "tile", None),
        P(),
        P(),
        P("tile"),
        P("tile"),
    )
    out_specs = P(None, "plane", "tile", None)
    return jax.shard_map(shards, mesh=mesh, in_specs=in_specs, out_specs=out_specs, check_vma=False)
```

```python
import jax
import jax.numpy as jnp
from jax import lax
from jax.experimental import pallas as pl
from jax.experimental.pallas import tpu as pltpu
from jax.sharding import PartitionSpec as P

ITERS = 2
LANES = 128
GROUP = 8
VMEM_LIMIT = 48 * 1024 * 1024


def params():
    return pltpu.CompilerParams(vmem_limit_bytes=VMEM_LIMIT)


def in_vmem():
    return pl.BlockSpec(memory_space=pltpu.VMEM)


def in_smem():
    return pl.BlockSpec(memory_space=pltpu.SMEM)


def split(value):
    high = value.astype(jnp.bfloat16)
    low = (value - high.astype(jnp.float32)).astype(jnp.bfloat16)
    return high, low


def payload_kernel(own, strip, extents, skews, to_core, to_chip, sems):
    strip_rows = strip.shape[2]
    tile = lax.axis_index("tile")
    low, high = slice(0, strip_rows), slice(strip_rows, 2 * strip_rows)

    def fill(up, down):
        pieces = []
        for c in range(strip.shape[0]):
            pieces += [
                (strip.at[c], up.at[c, :, low, :]),
                (own.at[c, :, own.shape[2] - strip_rows :, :], up.at[c, :, high, :]),
                (own.at[c, :, low, :], down.at[c, :, low, :]),
            ]
        copies = [pltpu.make_async_copy(source, target, sems.at[i]) for i, (source, target) in enumerate(pieces)]
        for copy in copies:
            copy.start()
        extent = jnp.where(tile == 0, 0, extents[0])
        column = lax.broadcasted_iota(jnp.int32, strip.shape, 3)
        down[:, :, high, :] = jnp.where(column < LANES, extent, skews[0]).astype(jnp.float32)
        for copy in copies:
            copy.wait()

    @pl.when(tile % 2 == 1)
    def _():
        fill(to_chip, to_core)

    @pl.when(tile % 2 == 0)
    def _():
        fill(to_core, to_chip)


def pack_kernel(to_core, to_chip, core, chip, _, windows, *, blocks):
    chans, _, row_count, voxels = core.shape
    half = row_count // 2
    block = voxels // blocks
    lane = lax.broadcasted_iota(jnp.int32, (1, LANES), 1)
    tall = lax.broadcasted_iota(jnp.int32, (half, voxels), 0)
    lower = lax.axis_index("tile") % 2 == 1

    def pick(low, high, c, part):
        at = slice(part * half, (part + 1) * half)
        return jnp.where(lower, low[c, 0, at, :], high[c, 0, at, :])

    def numbers(low, high):
        both = pick(low, high, 0, 1)[0:GROUP].astype(jnp.int32)
        return jnp.max(both[:, :LANES]), jnp.max(both[:, LANES:])

    extent, skew = numbers(to_core, to_chip)
    next_extent, next_skew = numbers(chip, core)
    for c in range(chans):
        turned = pltpu.roll(pick(core, chip, c, 0), skew, 1)
        top = pick(to_core, to_chip, c, 0)
        top = jnp.where(tall < extent, 0.5 * (top + turned), top)
        bottom = pick(to_chip, to_core, c, 1)
        turned = pltpu.roll(pick(to_chip, to_core, c, 0), next_skew, 1)
        after = chip[c, 0, :half, :]
        after = jnp.where(tall < next_extent, 0.5 * (after + turned), after)
        before = chip[c, 0, half:, :]
        rows = [jnp.where(lower, top, bottom), jnp.where(lower, bottom, top), jnp.where(lower, after, before)]
        rows = jnp.concatenate(rows, axis=0)
        for j in range(blocks):
            start = j * block - (LANES - LANES // 2) // 2
            window = pltpu.roll(rows, -start % voxels, 1)[:, :LANES]
            inside = (lane >= -start) & (lane < voxels - start)
            windows[c * blocks + j] = jnp.where(inside, window, 0.0)


def stages(row_count, half, lateral_half):
    def tiled(rows):
        return -(-rows // 16) * 16

    known = row_count + half
    skipped = half - 2 * ITERS * lateral_half
    out = [(known, known - 16, 0, 0), (half + 16, half, 0, 0)]
    read, rows, ahead = known + half - 16, known + half - 2 * skipped - 2 * lateral_half, skipped
    for k in range(1, 2 * ITERS):
        rows -= 2 * lateral_half
        out.append((read, tiled(rows), ahead, k % 2))
        read, ahead = tiled(rows), 0
    return out


def bands_kernel(axial, lateral, along_z, along_x, *along_y, spans, blocks):
    width = lateral.shape[1]
    chan = lax.axis_index("plane") // blocks
    taps = [lateral[chan, j] for j in range(width)]
    for j in range(axial.shape[1]):
        along_z[j] = jnp.full((GROUP, LANES), axial[chan, j], jnp.float32)
    offset = lax.broadcasted_iota(jnp.int32, (LANES, LANES), 0) - lax.broadcasted_iota(jnp.int32, (LANES, LANES), 1)

    def band(flipped, where, first):
        order = taps[::-1] if flipped else taps
        total = jnp.zeros((LANES, LANES), jnp.float32)
        for j in range(width):
            total = jnp.where(where == j + first, order[j], total)
        return split(total)

    for flipped in range(2):
        high, low = band(flipped, offset, -(width // 2))
        along_x[flipped, :LANES, :LANES] = high
        along_x[flipped, :LANES, LANES:] = low
        along_x[flipped, LANES:, :LANES] = high
        along_x[flipped, LANES:, LANES:] = jnp.zeros_like(low)
    made = {}
    for ref, (read, written, ahead, flipped) in zip(along_y, spans):
        if (ahead, flipped) not in made:
            made[ahead, flipped] = band(flipped, -offset, ahead)
        high, low = made[ahead, flipped]
        top, bottom = high[:written, :read], low[:written, :read]
        ref[:written] = jnp.concatenate([top, top], axis=1)
        ref[written:] = jnp.concatenate([bottom, jnp.zeros_like(bottom)], axis=1)


def planes_of(count):
    return [slice(q * LANES, (q + 1) * LANES) for q in range(count)]


def blur_x(values, band):
    out = []
    for q in range(0, len(values), 2):
        pair = jnp.concatenate(values[q : q + 2], axis=0)
        product = jnp.dot(jnp.concatenate(split(pair), axis=1), band, preferred_element_type=jnp.float32)
        product = product[:, :LANES] + product[:, LANES:]
        out += [product[: pair.shape[0] // 2], product[pair.shape[0] // 2 :]]
    return out


def blur_y(work, band, span):
    read, written = span[:2]
    for q in range(0, work.shape[1], 2 * LANES):
        pair = slice(q, q + 2 * LANES)
        both = jnp.concatenate(split(work[0:read, pair]), axis=0)
        product = jnp.dot(band[...], both, preferred_element_type=jnp.float32)
        work[0:written, pair] = product[:written] + product[written:]


def blur_z(values, axial, flipped):
    out = []
    for p in range(len(values)):
        total = None
        for q in range(len(values)):
            at = (p - q if flipped else q - p) + axial.shape[0] // 2
            if 0 <= at < axial.shape[0]:
                term = axial[at] * values[q]
                total = term if total is None else total + term
        out.append(total)
    return out


def quotient_along_z(work, joined, origin, axial, written, store):
    columns = planes_of(joined.shape[0])
    for row in range(0, written, GROUP):
        mixed = blur_z([work[row : row + GROUP, lanes] for lanes in columns], axial, False)
        quotient = []
        for p, blurred in enumerate(mixed):
            value = joined[p, row + origin : row + origin + GROUP, :]
            quotient.append(value / jnp.where(value > 0.0, blurred, 1.0))
        for lanes, value in zip(columns, blur_z(quotient, axial, True)):
            store(row, lanes, value)


def first_kernel(own, axial, x_bands, y_band, spread, joined, work, *, span, lateral_half):
    half = own.shape[1] // 3
    lower = lax.axis_index("tile") % 2 == 1
    for k in range(3):
        near, far = own[:, k * half : (k + 1) * half, :], own[:, (2 - k) * half : (3 - k) * half, :]
        joined[:, k * half : (k + 1) * half, :] = jnp.where(lower, near, far)
    planes = own.shape[0]
    columns = planes_of(planes)
    for lanes, value in zip(columns, blur_x([joined[p] for p in range(planes)], x_bands[0])):
        work[:, lanes] = value
    blur_y(work, y_band, span)

    def store(row, lanes, value):
        spread[row : row + GROUP, lanes] = value

    quotient_along_z(work, joined, lateral_half, axial, span[1], store)


def second_kernel(own, core, spread, axial, x_bands, *refs, spans, lateral_half, skipped, blocks):
    y_bands, (result, joined, border, work, estimate) = refs[: len(spans)], refs[len(spans) :]
    planes, half, _ = core.shape
    out_rows = 2 * half
    columns = planes_of(planes)
    lower = lax.axis_index("tile") % 2 == 1
    for place, piece in enumerate((core[...], *(own[:, k * half : (k + 1) * half, :] for k in range(3)))):
        at = jnp.where(lower, place, 3 - place) * half
        joined[:, pl.ds(pl.multiple_of(at, half), half), :] = piece

    border[:, 0:16, :] = jnp.where(lower, core[:, 0:16, :], own[:, half - 16 : half, :])
    border[:, 16:half, :] = jnp.where(lower, core[:, 16:half, :], core[:, 0 : half - 16, :])
    border[:, half:, :] = jnp.where(lower, own[:, 0:16, :], core[:, half - 16 :, :])
    for lanes, value in zip(columns, blur_x([border[p] for p in range(planes)], x_bands[0])):
        work[0 : half + 16, lanes] = value
    blur_y(work, y_bands[0], spans[0])
    first = jnp.where(lower, 0, spread.shape[0])

    def store(row, lanes, value):
        work[pl.ds(pl.multiple_of(first + row, GROUP), GROUP), lanes] = value

    held = [[work[row : row + GROUP, lanes] for lanes in columns] for row in range(0, half, GROUP)]
    for i, mixed in enumerate(held):
        row = i * GROUP
        quotient = []
        for p, blurred in enumerate(blur_z(mixed, axial, False)):
            value = border[p, row + lateral_half : row + lateral_half + GROUP, :]
            quotient.append(value / jnp.where(value > 0.0, blurred, 1.0))
        held[i] = blur_z(quotient, axial, True)
    for i, values in enumerate(held):
        for lanes, value in zip(columns, values):
            store(i * GROUP, lanes, value)
    others = jnp.where(lower, half, 0)
    work[pl.ds(pl.multiple_of(others, GROUP), spread.shape[0]), :] = spread[...]

    origin = skipped + lateral_half
    for sweep in range(ITERS):
        if sweep > 0:
            read, written = spans[2 * sweep][:2]
            source = [estimate[0:read, lanes] for lanes in columns]
            for lanes, value in zip(columns, blur_x(source, x_bands[0])):
                work[0:read, lanes] = value
            blur_y(work, y_bands[2 * sweep], spans[2 * sweep])
            origin += lateral_half

            def replace(row, lanes, value):
                work[row : row + GROUP, lanes] = value

            quotient_along_z(work, joined, origin, axial, written, replace)
        written = spans[2 * sweep + 1][1]
        blur_y(work, y_bands[2 * sweep + 1], spans[2 * sweep + 1])
        origin += lateral_half
        factor = blur_x([work[0:written, lanes] for lanes in columns], x_bands[1])
        for p, lanes in enumerate(columns):
            if sweep == 0:
                before = joined[p, origin : origin + written, :]
            else:
                before = estimate[2 * lateral_half : 2 * lateral_half + written, lanes]
            estimate[0:written, lanes] = before * factor[p]
    voxels = 2 * LANES // blocks
    parts = LANES // voxels
    tall = out_rows // parts
    side = (LANES - LANES // 2) // 2
    lane = lax.broadcasted_iota(jnp.int32, (1, LANES), 1)
    for p, lanes in enumerate(columns):
        packed = None
        for m in range(parts):
            piece = pltpu.roll(estimate[m * tall : (m + 1) * tall, lanes], (m * voxels - side) % LANES, 1)
            packed = piece if packed is None else jnp.where(lane < m * voxels, packed, piece)
        result[p] = packed


def unpack_kernel(received, out, *, blocks):
    chans, _, row_count, voxels = out.shape
    block = voxels // blocks
    parts = LANES // block
    tall = row_count // parts
    lane = lax.broadcasted_iota(jnp.int32, (1, LANES), 1)
    for c in range(chans):
        for column in range(0, voxels, LANES):
            first = c * blocks + column // block
            for m in range(parts):
                whole = None
                for i in range(parts):
                    value = received[first + i]
                    piece = value if i == m else pltpu.roll(value, (i - m) * block % LANES, 1)
                    whole = piece if whole is None else jnp.where(lane < i * block, whole, piece)
                out[c, 0, m * tall : (m + 1) * tall, column : column + LANES] = whole


def shards(observed, intersection_strip, axial_taps, lateral_taps, extents, section_skews):
    chans, _, row_count, voxels = observed.shape
    planes = lax.axis_size("plane")
    tiles = lax.axis_size("tile")
    half = row_count // 2
    blocks = planes // chans
    lateral_half = lateral_taps.shape[1] // 2
    skipped = half - 2 * ITERS * lateral_half
    window_rows = row_count + 2 * half
    spans = stages(row_count, half, lateral_half)
    cores = [(i, i ^ 1) for i in range(tiles)]
    chips = [pair for i in range(1, tiles - 1, 2) for pair in ((i, i + 1), (i + 1, i))]

    payload = jax.ShapeDtypeStruct((chans, 1, 2 * half, voxels), jnp.float32)
    to_core, to_chip = pl.pallas_call(
        payload_kernel,
        out_shape=(payload, payload),
        in_specs=[pl.BlockSpec(memory_space=pltpu.HBM)] * 2 + [in_smem()] * 2,
        out_specs=(in_vmem(), in_vmem()),
        scratch_shapes=[pltpu.SemaphoreType.DMA((3 * chans,))],
        compiler_params=params(),
        name="payload",
    )(*(pltpu.with_memory_space_constraint(array, pltpu.HBM) for array in (observed, intersection_strip)), extents, section_skews)
    chip = lax.ppermute(to_chip, "tile", chips)
    core = lax.ppermute(to_core, "tile", cores)
    bands = pl.pallas_call(
        lambda *refs: bands_kernel(*refs, spans=spans, blocks=blocks),
        out_shape=[
            jax.ShapeDtypeStruct((axial_taps.shape[1], GROUP, LANES), jnp.float32),
            jax.ShapeDtypeStruct((2, 2 * LANES, 2 * LANES), jnp.bfloat16),
        ]
        + [jax.ShapeDtypeStruct((2 * written, 2 * read), jnp.bfloat16) for read, written, _, _ in spans],
        in_specs=[in_smem()] * 2,
        out_specs=[in_vmem()] * (2 + len(spans)),
        cost_estimate=pl.CostEstimate(flops=1 << 20, bytes_accessed=1 << 20, transcendentals=0),
        compiler_params=params(),
        name="bands",
    )(axial_taps, lateral_taps)
    windows = pl.pallas_call(
        lambda *refs: pack_kernel(*refs, blocks=blocks),
        out_shape=jax.ShapeDtypeStruct((planes, row_count + half, LANES), jnp.float32),
        in_specs=[in_vmem()] * 4 + [pl.BlockSpec(memory_space=pl.ANY)],
        out_specs=in_vmem(),
        compiler_params=params(),
        name="pack",
    )(to_core, to_chip, core, chip, bands[0])
    windows = lax.all_to_all(windows, "plane", 0, 0, tiled=True)

    across = lax.ppermute(windows[:, :half, :], "tile", cores)
    along_z, along_x, *along_y = bands
    first, *rest = spans
    spread = pl.pallas_call(
        lambda *refs: first_kernel(*refs, span=first, lateral_half=lateral_half),
        out_shape=jax.ShapeDtypeStruct((first[1], planes * LANES), jnp.float32),
        in_specs=[in_vmem()] * 4,
        out_specs=in_vmem(),
        scratch_shapes=[
            pltpu.VMEM((planes, first[0], LANES), jnp.float32),
            pltpu.VMEM((first[0], planes * LANES), jnp.float32),
        ],
        cost_estimate=pl.CostEstimate(flops=1 << 29, bytes_accessed=1 << 20, transcendentals=0),
        compiler_params=params(),
        name="first",
    )(windows, along_z, along_x, along_y[0])
    result = pl.pallas_call(
        lambda *refs: second_kernel(*refs, spans=rest, lateral_half=lateral_half, skipped=skipped, blocks=blocks),
        out_shape=jax.ShapeDtypeStruct((planes, row_count * voxels // blocks // LANES, LANES), jnp.float32),
        in_specs=[in_vmem()] * (5 + len(rest)),
        out_specs=in_vmem(),
        scratch_shapes=[
            pltpu.VMEM((planes, window_rows, LANES), jnp.float32),
            pltpu.VMEM((planes, half + 16, LANES), jnp.float32),
            pltpu.VMEM((window_rows - 16, planes * LANES), jnp.float32),
            pltpu.VMEM((rest[1][1], planes * LANES), jnp.float32),
        ],
        compiler_params=params(),
        name="second",
    )(windows, across, spread, along_z, along_x, *along_y[1:])
    received = lax.all_to_all(result, "plane", 0, 0, tiled=True)
    return pl.pallas_call(
        lambda *refs: unpack_kernel(*refs, blocks=blocks),
        out_shape=jax.ShapeDtypeStruct(observed.shape, jnp.float32),
        in_specs=[in_vmem()],
        out_specs=in_vmem(),
        compiler_params=params(),
        name="unpack",
    )(received)


def solution(mesh):
    in_specs = (
        P(None, "plane", "tile", None),
        P(None, "plane", "tile", None),
        P(),
        P(),
        P("tile"),
        P("tile"),
    )
    out_specs = P(None, "plane", "tile", None)
    return jax.shard_map(shards, mesh=mesh, in_specs=in_specs, out_specs=out_specs, check_vma=False)
```

```python
import jax
import jax.numpy as jnp
from jax import lax
from jax.experimental import pallas as pl
from jax.experimental.pallas import tpu as pltpu
from jax.sharding import PartitionSpec as P

ITERS = 2
LANES = 128
GROUP = 8
VMEM_LIMIT = 48 * 1024 * 1024


def params():
    return pltpu.CompilerParams(vmem_limit_bytes=VMEM_LIMIT)


def in_vmem():
    return pl.BlockSpec(memory_space=pltpu.VMEM)


def in_smem():
    return pl.BlockSpec(memory_space=pltpu.SMEM)


def split(value):
    high = value.astype(jnp.bfloat16)
    low = (value - high.astype(jnp.float32)).astype(jnp.bfloat16)
    return high, low


def payload_kernel(own, strip, extents, skews, to_core, to_chip, sems):
    strip_rows = strip.shape[2]
    tile = lax.axis_index("tile")
    low, high = slice(0, strip_rows), slice(strip_rows, 2 * strip_rows)

    def fill(up, down):
        pieces = []
        for c in range(strip.shape[0]):
            pieces += [
                (strip.at[c], up.at[c, :, low, :]),
                (own.at[c, :, own.shape[2] - strip_rows :, :], up.at[c, :, high, :]),
                (own.at[c, :, low, :], down.at[c, :, low, :]),
            ]
        copies = [pltpu.make_async_copy(source, target, sems.at[i]) for i, (source, target) in enumerate(pieces)]
        for copy in copies:
            copy.start()
        extent = jnp.where(tile == 0, 0, extents[0])
        column = lax.broadcasted_iota(jnp.int32, strip.shape, 3)
        down[:, :, high, :] = jnp.where(column < LANES, extent, skews[0]).astype(jnp.float32)
        for copy in copies:
            copy.wait()

    @pl.when(tile % 2 == 1)
    def _():
        fill(to_chip, to_core)

    @pl.when(tile % 2 == 0)
    def _():
        fill(to_core, to_chip)


def pack_kernel(to_core, to_chip, core, chip, _, windows, *, blocks):
    chans, _, row_count, voxels = core.shape
    half = row_count // 2
    block = voxels // blocks
    lane = lax.broadcasted_iota(jnp.int32, (1, LANES), 1)
    tall = lax.broadcasted_iota(jnp.int32, (half, voxels), 0)
    lower = lax.axis_index("tile") % 2 == 1

    def pick(low, high, c, part):
        at = slice(part * half, (part + 1) * half)
        return jnp.where(lower, low[c, 0, at, :], high[c, 0, at, :])

    def numbers(low, high):
        both = pick(low, high, 0, 1)[0:GROUP].astype(jnp.int32)
        return jnp.max(both[:, :LANES]), jnp.max(both[:, LANES:])

    extent, skew = numbers(to_core, to_chip)
    next_extent, next_skew = numbers(chip, core)
    for c in range(chans):
        turned = pltpu.roll(pick(core, chip, c, 0), skew, 1)
        top = pick(to_core, to_chip, c, 0)
        top = jnp.where(tall < extent, 0.5 * (top + turned), top)
        bottom = pick(to_chip, to_core, c, 1)
        turned = pltpu.roll(pick(to_chip, to_core, c, 0), next_skew, 1)
        after = chip[c, 0, :half, :]
        after = jnp.where(tall < next_extent, 0.5 * (after + turned), after)
        before = chip[c, 0, half:, :]
        rows = [jnp.where(lower, top, bottom), jnp.where(lower, bottom, top), jnp.where(lower, after, before)]
        rows = jnp.concatenate(rows, axis=0)
        for j in range(blocks):
            start = j * block - (LANES - LANES // 2) // 2
            window = pltpu.roll(rows, -start % voxels, 1)[:, :LANES]
            inside = (lane >= -start) & (lane < voxels - start)
            windows[c * blocks + j] = jnp.where(inside, window, 0.0)


def stages(row_count, half, lateral_half):
    def tiled(rows):
        return -(-rows // 16) * 16

    known = row_count + half
    skipped = half - 2 * ITERS * lateral_half
    out = [(known, known - 16, 0, 0), (half + 16, half, 0, 0)]
    read, rows, ahead = known + half - 16, known + half - 2 * skipped - 2 * lateral_half, skipped
    for k in range(1, 2 * ITERS):
        rows -= 2 * lateral_half
        out.append((read, tiled(rows), ahead, k % 2))
        read, ahead = tiled(rows), 0
    return out


def bands_kernel(axial, lateral, along_z, along_x, *along_y, spans, blocks, order):
    width = lateral.shape[1]
    plane = lax.axis_index("plane")
    chan = jnp.int32(0)
    for place, owner in enumerate(order):
        chan = jnp.where(plane == owner, place // blocks, chan)
    taps = [lateral[chan, j] for j in range(width)]
    for j in range(axial.shape[1]):
        along_z[j] = jnp.full((GROUP, LANES), axial[chan, j], jnp.float32)
    offset = lax.broadcasted_iota(jnp.int32, (LANES, LANES), 0) - lax.broadcasted_iota(jnp.int32, (LANES, LANES), 1)

    def band(flipped, where, first):
        order = taps[::-1] if flipped else taps
        total = jnp.zeros((LANES, LANES), jnp.float32)
        for j in range(width):
            total = jnp.where(where == j + first, order[j], total)
        return split(total)

    for flipped in range(2):
        high, low = band(flipped, offset, -(width // 2))
        along_x[flipped, :LANES, :LANES] = high
        along_x[flipped, :LANES, LANES:] = low
        along_x[flipped, LANES:, :LANES] = high
        along_x[flipped, LANES:, LANES:] = jnp.zeros_like(low)
    made = {}
    for ref, (read, written, ahead, flipped) in zip(along_y, spans):
        if (ahead, flipped) not in made:
            made[ahead, flipped] = band(flipped, -offset, ahead)
        high, low = made[ahead, flipped]
        top, bottom = high[:written, :read], low[:written, :read]
        ref[:written] = jnp.concatenate([top, top], axis=1)
        ref[written:] = jnp.concatenate([bottom, jnp.zeros_like(bottom)], axis=1)


def planes_of(count):
    return [slice(q * LANES, (q + 1) * LANES) for q in range(count)]


def blur_x(values, band):
    out = []
    for q in range(0, len(values), 2):
        pair = jnp.concatenate(values[q : q + 2], axis=0)
        product = jnp.dot(jnp.concatenate(split(pair), axis=1), band, preferred_element_type=jnp.float32)
        product = product[:, :LANES] + product[:, LANES:]
        out += [product[: pair.shape[0] // 2], product[pair.shape[0] // 2 :]]
    return out


def blur_y(work, band, span):
    read, written = span[:2]
    for q in range(0, work.shape[1], 2 * LANES):
        pair = slice(q, q + 2 * LANES)
        both = jnp.concatenate(split(work[0:read, pair]), axis=0)
        product = jnp.dot(band[...], both, preferred_element_type=jnp.float32)
        work[0:written, pair] = product[:written] + product[written:]


def blur_z(values, axial, flipped, order):
    out = []
    for p in range(len(values)):
        total = None
        for q in range(len(values)):
            at = (order[p] - order[q] if flipped else order[q] - order[p]) + axial.shape[0] // 2
            if 0 <= at < axial.shape[0]:
                term = axial[at] * values[q]
                total = term if total is None else total + term
        out.append(total)
    return out


def quotient_along_z(work, joined, origin, axial, order, written, store):
    columns = planes_of(joined.shape[0])
    for row in range(0, written, GROUP):
        mixed = blur_z([work[row : row + GROUP, lanes] for lanes in columns], axial, False, order)
        quotient = []
        for p, blurred in enumerate(mixed):
            value = joined[p, row + origin : row + origin + GROUP, :]
            quotient.append(value / jnp.where(value > 0.0, blurred, 1.0))
        for lanes, value in zip(columns, blur_z(quotient, axial, True, order)):
            store(row, lanes, value)


def first_kernel(own, axial, x_bands, y_band, spread, joined, work, *, span, lateral_half, order):
    half = own.shape[1] // 3
    lower = lax.axis_index("tile") % 2 == 1
    for k in range(3):
        near, far = own[:, k * half : (k + 1) * half, :], own[:, (2 - k) * half : (3 - k) * half, :]
        joined[:, k * half : (k + 1) * half, :] = jnp.where(lower, near, far)
    planes = own.shape[0]
    columns = planes_of(planes)
    for lanes, value in zip(columns, blur_x([joined[p] for p in range(planes)], x_bands[0])):
        work[:, lanes] = value
    blur_y(work, y_band, span)

    def store(row, lanes, value):
        spread[row : row + GROUP, lanes] = value

    quotient_along_z(work, joined, lateral_half, axial, order, span[1], store)


def second_kernel(own, core, spread, axial, x_bands, *refs, spans, lateral_half, skipped, blocks, order, sent):
    y_bands, (result, joined, border, work, estimate) = refs[: len(spans)], refs[len(spans) :]
    planes, half, _ = core.shape
    out_rows = 2 * half
    columns = planes_of(planes)
    lower = lax.axis_index("tile") % 2 == 1
    for place, piece in enumerate((core[...], *(own[:, k * half : (k + 1) * half, :] for k in range(3)))):
        at = jnp.where(lower, place, 3 - place) * half
        joined[:, pl.ds(pl.multiple_of(at, half), half), :] = piece

    border[:, 0:16, :] = jnp.where(lower, core[:, 0:16, :], own[:, half - 16 : half, :])
    border[:, 16:half, :] = jnp.where(lower, core[:, 16:half, :], core[:, 0 : half - 16, :])
    border[:, half:, :] = jnp.where(lower, own[:, 0:16, :], core[:, half - 16 :, :])
    for lanes, value in zip(columns, blur_x([border[p] for p in range(planes)], x_bands[0])):
        work[0 : half + 16, lanes] = value
    blur_y(work, y_bands[0], spans[0])
    first = jnp.where(lower, 0, spread.shape[0])

    def store(row, lanes, value):
        work[pl.ds(pl.multiple_of(first + row, GROUP), GROUP), lanes] = value

    held = [[work[row : row + GROUP, lanes] for lanes in columns] for row in range(0, half, GROUP)]
    for i, mixed in enumerate(held):
        row = i * GROUP
        quotient = []
        for p, blurred in enumerate(blur_z(mixed, axial, False, order)):
            value = border[p, row + lateral_half : row + lateral_half + GROUP, :]
            quotient.append(value / jnp.where(value > 0.0, blurred, 1.0))
        held[i] = blur_z(quotient, axial, True, order)
    for i, values in enumerate(held):
        for lanes, value in zip(columns, values):
            store(i * GROUP, lanes, value)
    others = jnp.where(lower, half, 0)
    work[pl.ds(pl.multiple_of(others, GROUP), spread.shape[0]), :] = spread[...]

    origin = skipped + lateral_half
    for sweep in range(ITERS):
        if sweep > 0:
            read, written = spans[2 * sweep][:2]
            source = [estimate[0:read, lanes] for lanes in columns]
            for lanes, value in zip(columns, blur_x(source, x_bands[0])):
                work[0:read, lanes] = value
            blur_y(work, y_bands[2 * sweep], spans[2 * sweep])
            origin += lateral_half

            def replace(row, lanes, value):
                work[row : row + GROUP, lanes] = value

            quotient_along_z(work, joined, origin, axial, order, written, replace)
        written = spans[2 * sweep + 1][1]
        blur_y(work, y_bands[2 * sweep + 1], spans[2 * sweep + 1])
        origin += lateral_half
        factor = blur_x([work[0:written, lanes] for lanes in columns], x_bands[1])
        for p, lanes in enumerate(columns):
            if sweep == 0:
                before = joined[p, origin : origin + written, :]
            else:
                before = estimate[2 * lateral_half : 2 * lateral_half + written, lanes]
            estimate[0:written, lanes] = before * factor[p]
    voxels = 2 * LANES // blocks
    parts = LANES // voxels
    tall = out_rows // parts
    side = (LANES - LANES // 2) // 2
    lane = lax.broadcasted_iota(jnp.int32, (1, LANES), 1)
    for p, lanes in enumerate(columns):
        packed = None
        for m in range(parts):
            piece = pltpu.roll(estimate[m * tall : (m + 1) * tall, lanes], (m * voxels - side) % LANES, 1)
            packed = piece if packed is None else jnp.where(lane < m * voxels, packed, piece)
        result[sent.index(order[p])] = packed


def unpack_kernel(received, out, *, blocks, order, sent):
    chans, _, row_count, voxels = out.shape
    block = voxels // blocks
    parts = LANES // block
    tall = row_count // parts
    lane = lax.broadcasted_iota(jnp.int32, (1, LANES), 1)
    for c in range(chans):
        for column in range(0, voxels, LANES):
            first = c * blocks + column // block
            for m in range(parts):
                whole = None
                for i in range(parts):
                    value = received[sent.index(order[first + i])]
                    piece = value if i == m else pltpu.roll(value, (i - m) * block % LANES, 1)
                    whole = piece if whole is None else jnp.where(lane < i * block, whole, piece)
                out[c, 0, m * tall : (m + 1) * tall, column : column + LANES] = whole


def group_orders(planes):
    if planes == 8:
        return [5, 1, 0, 2, 7, 4, 3, 6], [5, 1, 0, 2, 7, 4, 3, 6]
    return list(range(planes)), list(range(planes))


def shards(observed, intersection_strip, axial_taps, lateral_taps, extents, section_skews):
    chans, _, row_count, voxels = observed.shape
    planes = lax.axis_size("plane")
    tiles = lax.axis_size("tile")
    half = row_count // 2
    blocks = planes // chans
    order, sent = group_orders(planes)
    lateral_half = lateral_taps.shape[1] // 2
    skipped = half - 2 * ITERS * lateral_half
    window_rows = row_count + 2 * half
    spans = stages(row_count, half, lateral_half)
    cores = [(i, i ^ 1) for i in range(tiles)]
    chips = [pair for i in range(1, tiles - 1, 2) for pair in ((i, i + 1), (i + 1, i))]

    payload = jax.ShapeDtypeStruct((chans, 1, 2 * half, voxels), jnp.float32)
    to_core, to_chip = pl.pallas_call(
        payload_kernel,
        out_shape=(payload, payload),
        in_specs=[pl.BlockSpec(memory_space=pltpu.HBM)] * 2 + [in_smem()] * 2,
        out_specs=(in_vmem(), in_vmem()),
        scratch_shapes=[pltpu.SemaphoreType.DMA((3 * chans,))],
        compiler_params=params(),
        name="payload",
    )(*(pltpu.with_memory_space_constraint(array, pltpu.HBM) for array in (observed, intersection_strip)), extents, section_skews)
    chip = lax.ppermute(to_chip, "tile", chips)
    core = lax.ppermute(to_core, "tile", cores)
    bands = pl.pallas_call(
        lambda *refs: bands_kernel(*refs, spans=spans, blocks=blocks, order=order),
        out_shape=[
            jax.ShapeDtypeStruct((axial_taps.shape[1], GROUP, LANES), jnp.float32),
            jax.ShapeDtypeStruct((2, 2 * LANES, 2 * LANES), jnp.bfloat16),
        ]
        + [jax.ShapeDtypeStruct((2 * written, 2 * read), jnp.bfloat16) for read, written, _, _ in spans],
        in_specs=[in_smem()] * 2,
        out_specs=[in_vmem()] * (2 + len(spans)),
        cost_estimate=pl.CostEstimate(flops=1 << 20, bytes_accessed=1 << 20, transcendentals=0),
        compiler_params=params(),
        name="bands",
    )(axial_taps, lateral_taps)
    windows = pl.pallas_call(
        lambda *refs: pack_kernel(*refs, blocks=blocks),
        out_shape=jax.ShapeDtypeStruct((planes, row_count + half, LANES), jnp.float32),
        in_specs=[in_vmem()] * 4 + [pl.BlockSpec(memory_space=pl.ANY)],
        out_specs=in_vmem(),
        compiler_params=params(),
        name="pack",
    )(to_core, to_chip, core, chip, bands[0])
    windows = lax.all_to_all(windows, "plane", 0, 0, axis_index_groups=[order], tiled=True)

    across = lax.ppermute(windows[:, :half, :], "tile", cores)
    along_z, along_x, *along_y = bands
    first, *rest = spans
    spread = pl.pallas_call(
        lambda *refs: first_kernel(*refs, span=first, lateral_half=lateral_half, order=order),
        out_shape=jax.ShapeDtypeStruct((first[1], planes * LANES), jnp.float32),
        in_specs=[in_vmem()] * 4,
        out_specs=in_vmem(),
        scratch_shapes=[
            pltpu.VMEM((planes, first[0], LANES), jnp.float32),
            pltpu.VMEM((first[0], planes * LANES), jnp.float32),
        ],
        cost_estimate=pl.CostEstimate(flops=1 << 29, bytes_accessed=1 << 20, transcendentals=0),
        compiler_params=params(),
        name="first",
    )(windows, along_z, along_x, along_y[0])
    result = pl.pallas_call(
        lambda *refs: second_kernel(
            *refs,
            spans=rest,
            lateral_half=lateral_half,
            skipped=skipped,
            blocks=blocks,
            order=order,
            sent=sent,
        ),
        out_shape=jax.ShapeDtypeStruct((planes, row_count * voxels // blocks // LANES, LANES), jnp.float32),
        in_specs=[in_vmem()] * (5 + len(rest)),
        out_specs=in_vmem(),
        scratch_shapes=[
            pltpu.VMEM((planes, window_rows, LANES), jnp.float32),
            pltpu.VMEM((planes, half + 16, LANES), jnp.float32),
            pltpu.VMEM((window_rows - 16, planes * LANES), jnp.float32),
            pltpu.VMEM((rest[1][1], planes * LANES), jnp.float32),
        ],
        compiler_params=params(),
        name="second",
    )(windows, across, spread, along_z, along_x, *along_y[1:])
    received = lax.all_to_all(result, "plane", 0, 0, axis_index_groups=[sent], tiled=True)
    return pl.pallas_call(
        lambda *refs: unpack_kernel(*refs, blocks=blocks, order=order, sent=sent),
        out_shape=jax.ShapeDtypeStruct(observed.shape, jnp.float32),
        in_specs=[in_vmem()],
        out_specs=in_vmem(),
        compiler_params=params(),
        name="unpack",
    )(received)


def solution(mesh):
    in_specs = (
        P(None, "plane", "tile", None),
        P(None, "plane", "tile", None),
        P(),
        P(),
        P("tile"),
        P("tile"),
    )
    out_specs = P(None, "plane", "tile", None)
    return jax.shard_map(shards, mesh=mesh, in_specs=in_specs, out_specs=out_specs, check_vma=False)
```

```python
import jax
import jax.numpy as jnp
from jax import lax
from jax.experimental import pallas as pl
from jax.experimental.pallas import tpu as pltpu
from jax.sharding import PartitionSpec as P

ITERS = 2
LANES = 128
GROUP = 8
VMEM_LIMIT = 48 * 1024 * 1024


def params():
    return pltpu.CompilerParams(vmem_limit_bytes=VMEM_LIMIT)


def in_vmem():
    return pl.BlockSpec(memory_space=pltpu.VMEM)


def in_smem():
    return pl.BlockSpec(memory_space=pltpu.SMEM)


def split(value):
    high = value.astype(jnp.bfloat16)
    low = (value - high.astype(jnp.float32)).astype(jnp.bfloat16)
    return high, low


def payload_kernel(own, strip, extents, skews, to_core, to_chip, sems):
    strip_rows = strip.shape[2]
    tile = lax.axis_index("tile")
    low, high = slice(0, strip_rows), slice(strip_rows, 2 * strip_rows)

    def fill(up, down):
        pieces = []
        for c in range(strip.shape[0]):
            pieces += [
                (strip.at[c], up.at[c, :, low, :]),
                (own.at[c, :, own.shape[2] - strip_rows :, :], up.at[c, :, high, :]),
                (own.at[c, :, low, :], down.at[c, :, low, :]),
            ]
        copies = [pltpu.make_async_copy(source, target, sems.at[i]) for i, (source, target) in enumerate(pieces)]
        for copy in copies:
            copy.start()
        extent = jnp.where(tile == 0, 0, extents[0])
        column = lax.broadcasted_iota(jnp.int32, strip.shape, 3)
        down[:, :, high, :] = jnp.where(column < LANES, extent, skews[0]).astype(jnp.float32)
        for copy in copies:
            copy.wait()

    @pl.when(tile % 2 == 1)
    def _():
        fill(to_chip, to_core)

    @pl.when(tile % 2 == 0)
    def _():
        fill(to_core, to_chip)


def pack_kernel(to_core, to_chip, core, chip, _, windows, *, blocks):
    chans, _, row_count, voxels = core.shape
    half = row_count // 2
    block = voxels // blocks
    lane = lax.broadcasted_iota(jnp.int32, (1, LANES), 1)
    tall = lax.broadcasted_iota(jnp.int32, (half, voxels), 0)
    lower = lax.axis_index("tile") % 2 == 1

    def pick(low, high, c, part):
        at = slice(part * half, (part + 1) * half)
        return jnp.where(lower, low[c, 0, at, :], high[c, 0, at, :])

    def numbers(low, high):
        both = pick(low, high, 0, 1)[0:GROUP].astype(jnp.int32)
        return jnp.max(both[:, :LANES]), jnp.max(both[:, LANES:])

    extent, skew = numbers(to_core, to_chip)
    next_extent, next_skew = numbers(chip, core)
    for c in range(chans):
        turned = pltpu.roll(pick(core, chip, c, 0), skew, 1)
        top = pick(to_core, to_chip, c, 0)
        top = jnp.where(tall < extent, 0.5 * (top + turned), top)
        bottom = pick(to_chip, to_core, c, 1)
        turned = pltpu.roll(pick(to_chip, to_core, c, 0), next_skew, 1)
        after = chip[c, 0, :half, :]
        after = jnp.where(tall < next_extent, 0.5 * (after + turned), after)
        before = chip[c, 0, half:, :]
        rows = [jnp.where(lower, top, bottom), jnp.where(lower, bottom, top), jnp.where(lower, after, before)]
        rows = jnp.concatenate(rows, axis=0)
        for j in range(blocks):
            start = j * block - (LANES - LANES // 2) // 2
            window = pltpu.roll(rows, -start % voxels, 1)[:, :LANES]
            inside = (lane >= -start) & (lane < voxels - start)
            windows[c * blocks + j] = jnp.where(inside, window, 0.0)


def stages(row_count, half, skipped):
    known = row_count + half
    held = [(known, known - 16, 0, 0), (known - 16, known - 32, 0, 1)]
    border = [(half + 16, half, 0, 0), (half + 16, half, 0, 1)]
    return held, border, [(known, known - 16, skipped, 0), (known - 16, row_count, 0, 1)]


def bands_kernel(axial, lateral, along_z, along_x, *along_y, spans, blocks, order):
    width = lateral.shape[1]
    plane = lax.axis_index("plane")
    chan = jnp.int32(0)
    for place, owner in enumerate(order):
        chan = jnp.where(plane == owner, place // blocks, chan)
    taps = [lateral[chan, j] for j in range(width)]
    for j in range(axial.shape[1]):
        along_z[j] = jnp.full((GROUP, LANES), axial[chan, j], jnp.float32)
    offset = lax.broadcasted_iota(jnp.int32, (LANES, LANES), 0) - lax.broadcasted_iota(jnp.int32, (LANES, LANES), 1)

    def band(flipped, where, first):
        order = taps[::-1] if flipped else taps
        total = jnp.zeros((LANES, LANES), jnp.float32)
        for j in range(width):
            total = jnp.where(where == j + first, order[j], total)
        return split(total)

    for flipped in range(2):
        high, low = band(flipped, offset, -(width // 2))
        along_x[flipped, :LANES, :LANES] = high
        along_x[flipped, :LANES, LANES:] = low
        along_x[flipped, LANES:, :LANES] = high
        along_x[flipped, LANES:, LANES:] = jnp.zeros_like(low)
    made = {}
    for ref, (read, written, ahead, flipped) in zip(along_y, spans):
        if (ahead, flipped) not in made:
            made[ahead, flipped] = band(flipped, -offset, ahead)
        high, low = made[ahead, flipped]
        top, bottom = high[:written, :read], low[:written, :read]
        ref[:written] = jnp.concatenate([top, top], axis=1)
        ref[written:] = jnp.concatenate([bottom, jnp.zeros_like(bottom)], axis=1)


def planes_of(count):
    return [slice(q * LANES, (q + 1) * LANES) for q in range(count)]


def blur_x(values, band):
    out = []
    for q in range(0, len(values), 2):
        pair = jnp.concatenate(values[q : q + 2], axis=0)
        product = jnp.dot(jnp.concatenate(split(pair), axis=1), band, preferred_element_type=jnp.float32)
        product = product[:, :LANES] + product[:, LANES:]
        out += [product[: pair.shape[0] // 2], product[pair.shape[0] // 2 :]]
    return out


def blur_y(work, band, span):
    read, written = span[:2]
    for q in range(0, work.shape[1], 2 * LANES):
        pair = slice(q, q + 2 * LANES)
        both = jnp.concatenate(split(work[0:read, pair]), axis=0)
        product = jnp.dot(band[...], both, preferred_element_type=jnp.float32)
        work[0:written, pair] = product[:written] + product[written:]


def blur_z(values, axial, flipped, order):
    out = []
    for p in range(len(values)):
        total = None
        for q in range(len(values)):
            at = (order[p] - order[q] if flipped else order[q] - order[p]) + axial.shape[0] // 2
            if 0 <= at < axial.shape[0]:
                term = axial[at] * values[q]
                total = term if total is None else total + term
        out.append(total)
    return out


def quotient_along_z(work, joined, origin, axial, order, written, store):
    columns = planes_of(joined.shape[0])
    for row in range(0, written, GROUP):
        mixed = blur_z([work[row : row + GROUP, lanes] for lanes in columns], axial, False, order)
        quotient = []
        for p, blurred in enumerate(mixed):
            value = joined[p, row + origin : row + origin + GROUP, :]
            quotient.append(value / jnp.where(value > 0.0, blurred, 1.0))
        for lanes, value in zip(columns, blur_z(quotient, axial, True, order)):
            store(row, lanes, value)


def first_kernel(own, axial, x_bands, *refs, spans, lateral_half, order):
    y_bands, (edge, estimate, joined, work) = refs[:2], refs[2:]
    half = own.shape[1] // 3
    lower = lax.axis_index("tile") % 2 == 1
    for k in range(3):
        near, far = own[:, k * half : (k + 1) * half, :], own[:, (2 - k) * half : (3 - k) * half, :]
        joined[:, k * half : (k + 1) * half, :] = jnp.where(lower, near, far)
    planes = own.shape[0]
    columns = planes_of(planes)
    for lanes, value in zip(columns, blur_x([joined[p] for p in range(planes)], x_bands[0])):
        work[:, lanes] = value
    blur_y(work, y_bands[0], spans[0])

    def store(row, lanes, value):
        work[row : row + GROUP, lanes] = value

    rows = spans[0][1]
    quotient_along_z(work, joined, lateral_half, axial, order, rows, store)
    edge[...] = jnp.where(lower, work[0:16, :], work[rows - 16 : rows, :])
    blur_y(work, y_bands[1], spans[1])
    rows = spans[1][1]
    factor = blur_x([work[0:rows, lanes] for lanes in columns], x_bands[1])
    for p, lanes in enumerate(columns):
        estimate[:, lanes] = joined[p, 2 * lateral_half : 2 * lateral_half + rows, :] * factor[p]


def second_kernel(own, core, edge, held, axial, x_bands, *refs, spans, lateral_half, blocks, order, sent):
    y_bands, (result, joined, border, work, estimate) = refs[: len(spans)], refs[len(spans) :]
    planes, half, _ = core.shape
    out_rows = 2 * half
    columns = planes_of(planes)
    lower = lax.axis_index("tile") % 2 == 1
    for place, piece in enumerate((core[...], *(own[:, k * half : (k + 1) * half, :] for k in range(3)))):
        at = jnp.where(lower, place, 3 - place) * half
        joined[:, pl.ds(pl.multiple_of(at, half), half), :] = piece

    border[:, 0:half, :] = jnp.where(lower, core[...], own[:, 0:half, :])
    border[:, half:, :] = jnp.where(lower, own[:, 0:half, :], core[...])
    read, rows = spans[0][:2]
    source = [jnp.where(lower, border[p, 0:read, :], border[p, 16 : 16 + read, :]) for p in range(planes)]
    for lanes, value in zip(columns, blur_x(source, x_bands[0])):
        work[0:read, lanes] = value
    blur_y(work, y_bands[0], spans[0])
    quotients = []
    for row in range(0, rows, GROUP):
        quotient = []
        for p, blurred in enumerate(blur_z([work[row : row + GROUP, lanes] for lanes in columns], axial, False, order)):
            at = row + lateral_half
            value = jnp.where(lower, border[p, at : at + GROUP, :], border[p, at + 16 : at + 16 + GROUP, :])
            quotient.append(value / jnp.where(value > 0.0, blurred, 1.0))
        quotients.append(blur_z(quotient, axial, True, order))
    for lanes, values in zip(columns, zip(*quotients)):
        near, far = edge[:, lanes], jnp.concatenate(values, axis=0)
        work[0:16, lanes] = jnp.where(lower, far[0:16], near)
        work[16:rows, lanes] = jnp.where(lower, far[16:], far[: rows - 16])
        work[rows:read, lanes] = jnp.where(lower, near, far[rows - 16 :])
    blur_y(work, y_bands[1], spans[1])
    factor = blur_x([work[0:rows, lanes] for lanes in columns], x_bands[1])
    at = jnp.where(lower, 0, held.shape[0])
    others = jnp.where(lower, rows, 0)
    estimate[pl.ds(pl.multiple_of(others, 16), held.shape[0]), :] = held[...]
    for p, lanes in enumerate(columns):
        value = border[p, 2 * lateral_half : 2 * lateral_half + rows, :] * factor[p]
        estimate[pl.ds(pl.multiple_of(at, 16), rows), lanes] = value

    read, written = spans[2][:2]
    for lanes, value in zip(columns, blur_x([estimate[0:read, lanes] for lanes in columns], x_bands[0])):
        work[0:read, lanes] = value
    blur_y(work, y_bands[2], spans[2])

    def replace(row, lanes, value):
        work[row : row + GROUP, lanes] = value

    quotient_along_z(work, joined, half - lateral_half, axial, order, written, replace)
    blur_y(work, y_bands[3], spans[3])
    factor = blur_x([work[0:out_rows, lanes] for lanes in columns], x_bands[1])
    voxels = 2 * LANES // blocks
    parts = LANES // voxels
    tall = out_rows // parts
    side = (LANES - LANES // 2) // 2
    lane = lax.broadcasted_iota(jnp.int32, (1, LANES), 1)
    first = half - 2 * lateral_half
    for p, lanes in enumerate(columns):
        value = estimate[first : first + out_rows, lanes] * factor[p]
        packed = None
        for m in range(parts):
            piece = pltpu.roll(value[m * tall : (m + 1) * tall], (m * voxels - side) % LANES, 1)
            packed = piece if packed is None else jnp.where(lane < m * voxels, packed, piece)
        result[sent.index(order[p])] = packed


def unpack_kernel(received, out, *, blocks, order, sent):
    chans, _, row_count, voxels = out.shape
    block = voxels // blocks
    parts = LANES // block
    tall = row_count // parts
    lane = lax.broadcasted_iota(jnp.int32, (1, LANES), 1)
    for c in range(chans):
        for column in range(0, voxels, LANES):
            first = c * blocks + column // block
            for m in range(parts):
                whole = None
                for i in range(parts):
                    value = received[sent.index(order[first + i])]
                    piece = value if i == m else pltpu.roll(value, (i - m) * block % LANES, 1)
                    whole = piece if whole is None else jnp.where(lane < i * block, whole, piece)
                out[c, 0, m * tall : (m + 1) * tall, column : column + LANES] = whole


def group_orders(planes):
    if planes == 8:
        return [5, 0, 4, 7, 1, 3, 2, 6], [5, 1, 0, 4, 7, 2, 3, 6]
    return list(range(planes)), list(range(planes))


def shards(observed, intersection_strip, axial_taps, lateral_taps, extents, section_skews):
    chans, _, row_count, voxels = observed.shape
    planes = lax.axis_size("plane")
    tiles = lax.axis_size("tile")
    half = row_count // 2
    blocks = planes // chans
    order, sent = group_orders(planes)
    lateral_half = lateral_taps.shape[1] // 2
    skipped = half - 2 * ITERS * lateral_half
    window_rows = row_count + 2 * half
    held_spans, border_spans, whole_spans = stages(row_count, half, skipped)
    spans = held_spans + border_spans + whole_spans
    cores = [(i, i ^ 1) for i in range(tiles)]
    chips = [pair for i in range(1, tiles - 1, 2) for pair in ((i, i + 1), (i + 1, i))]

    payload = jax.ShapeDtypeStruct((chans, 1, 2 * half, voxels), jnp.float32)
    to_core, to_chip = pl.pallas_call(
        payload_kernel,
        out_shape=(payload, payload),
        in_specs=[pl.BlockSpec(memory_space=pltpu.HBM)] * 2 + [in_smem()] * 2,
        out_specs=(in_vmem(), in_vmem()),
        scratch_shapes=[pltpu.SemaphoreType.DMA((3 * chans,))],
        compiler_params=params(),
        name="payload",
    )(*(pltpu.with_memory_space_constraint(array, pltpu.HBM) for array in (observed, intersection_strip)), extents, section_skews)
    chip = lax.ppermute(to_chip, "tile", chips)
    core = lax.ppermute(to_core, "tile", cores)
    bands = pl.pallas_call(
        lambda *refs: bands_kernel(*refs, spans=spans, blocks=blocks, order=order),
        out_shape=[
            jax.ShapeDtypeStruct((axial_taps.shape[1], GROUP, LANES), jnp.float32),
            jax.ShapeDtypeStruct((2, 2 * LANES, 2 * LANES), jnp.bfloat16),
        ]
        + [jax.ShapeDtypeStruct((2 * written, 2 * read), jnp.bfloat16) for read, written, _, _ in spans],
        in_specs=[in_smem()] * 2,
        out_specs=[in_vmem()] * (2 + len(spans)),
        cost_estimate=pl.CostEstimate(flops=1 << 20, bytes_accessed=1 << 20, transcendentals=0),
        compiler_params=params(),
        name="bands",
    )(axial_taps, lateral_taps)
    windows = pl.pallas_call(
        lambda *refs: pack_kernel(*refs, blocks=blocks),
        out_shape=jax.ShapeDtypeStruct((planes, row_count + half, LANES), jnp.float32),
        in_specs=[in_vmem()] * 4 + [pl.BlockSpec(memory_space=pl.ANY)],
        out_specs=in_vmem(),
        compiler_params=params(),
        name="pack",
    )(to_core, to_chip, core, chip, bands[0])
    windows = lax.all_to_all(windows, "plane", 0, 0, axis_index_groups=[order], tiled=True)

    across = lax.ppermute(windows[:, :half, :], "tile", cores)
    along_z, along_x, *along_y = bands
    known = row_count + half
    edge, held = pl.pallas_call(
        lambda *refs: first_kernel(*refs, spans=held_spans, lateral_half=lateral_half, order=order),
        out_shape=(
            jax.ShapeDtypeStruct((16, planes * LANES), jnp.float32),
            jax.ShapeDtypeStruct((held_spans[1][1], planes * LANES), jnp.float32),
        ),
        in_specs=[in_vmem()] * 5,
        out_specs=(in_vmem(), in_vmem()),
        scratch_shapes=[
            pltpu.VMEM((planes, known, LANES), jnp.float32),
            pltpu.VMEM((known, planes * LANES), jnp.float32),
        ],
        cost_estimate=pl.CostEstimate(flops=1 << 29, bytes_accessed=1 << 20, transcendentals=0),
        compiler_params=params(),
        name="first",
    )(windows, along_z, along_x, *along_y[:2])
    result = pl.pallas_call(
        lambda *refs: second_kernel(
            *refs,
            spans=border_spans + whole_spans,
            lateral_half=lateral_half,
            blocks=blocks,
            order=order,
            sent=sent,
        ),
        out_shape=jax.ShapeDtypeStruct((planes, row_count * voxels // blocks // LANES, LANES), jnp.float32),
        in_specs=[in_vmem()] * 10,
        out_specs=in_vmem(),
        scratch_shapes=[
            pltpu.VMEM((planes, window_rows, LANES), jnp.float32),
            pltpu.VMEM((planes, row_count, LANES), jnp.float32),
            pltpu.VMEM((known, planes * LANES), jnp.float32),
            pltpu.VMEM((known, planes * LANES), jnp.float32),
        ],
        compiler_params=params(),
        name="second",
    )(windows, across, edge, held, along_z, along_x, *along_y[2:])
    received = lax.all_to_all(result, "plane", 0, 0, axis_index_groups=[sent], tiled=True)
    return pl.pallas_call(
        lambda *refs: unpack_kernel(*refs, blocks=blocks, order=order, sent=sent),
        out_shape=jax.ShapeDtypeStruct(observed.shape, jnp.float32),
        in_specs=[in_vmem()],
        out_specs=in_vmem(),
        compiler_params=params(),
        name="unpack",
    )(received)


def solution(mesh):
    in_specs = (
        P(None, "plane", "tile", None),
        P(None, "plane", "tile", None),
        P(),
        P(),
        P("tile"),
        P("tile"),
    )
    out_specs = P(None, "plane", "tile", None)
    return jax.shard_map(shards, mesh=mesh, in_specs=in_specs, out_specs=out_specs, check_vma=False)
```

```python
import jax
import jax.numpy as jnp
from jax import lax
from jax.experimental import pallas as pl
from jax.experimental.pallas import tpu as pltpu
from jax.sharding import PartitionSpec as P

ITERS = 2
LANES = 128
GROUP = 8
VMEM_LIMIT = 48 * 1024 * 1024


def params():
    return pltpu.CompilerParams(vmem_limit_bytes=VMEM_LIMIT)


def in_vmem():
    return pl.BlockSpec(memory_space=pltpu.VMEM)


def in_smem():
    return pl.BlockSpec(memory_space=pltpu.SMEM)


def payload_kernel(own, strip, extents, skews, to_core, to_chip, sems):
    strip_rows = strip.shape[2]
    tile = lax.axis_index("tile")
    low, high = slice(0, strip_rows), slice(strip_rows, 2 * strip_rows)

    def fill(up, down):
        pieces = []
        for c in range(strip.shape[0]):
            pieces += [
                (strip.at[c], up.at[c, :, low, :]),
                (own.at[c, :, own.shape[2] - strip_rows :, :], up.at[c, :, high, :]),
                (own.at[c, :, low, :], down.at[c, :, low, :]),
            ]
        copies = [pltpu.make_async_copy(source, target, sems.at[i]) for i, (source, target) in enumerate(pieces)]
        for copy in copies:
            copy.start()
        extent = jnp.where(tile == 0, 0, extents[0])
        column = lax.broadcasted_iota(jnp.int32, strip.shape, 3)
        down[:, :, high, :] = jnp.where(column < LANES, extent, skews[0]).astype(jnp.float32)
        for copy in copies:
            copy.wait()

    @pl.when(tile % 2 == 1)
    def _():
        fill(to_chip, to_core)

    @pl.when(tile % 2 == 0)
    def _():
        fill(to_core, to_chip)


def pack_kernel(to_core, to_chip, core, chip, _, windows, rows, *, reach, blocks, row_blocks):
    chans, _, row_count, voxels = core.shape
    strip_rows = row_count // 2
    lane = lax.broadcasted_iota(jnp.int32, (1, LANES), 1)
    tall = lax.broadcasted_iota(jnp.int32, (strip_rows, voxels), 0)
    edge = LANES // 4
    block_rows = row_count // row_blocks
    window_rows = block_rows + 2 * reach
    lower = lax.axis_index("tile") % 2 == 1

    def pick(low, high, c, part):
        at = slice(part * strip_rows, (part + 1) * strip_rows)
        return jnp.where(lower, low[c, 0, at, :], high[c, 0, at, :])

    def numbers(low, high):
        both = pick(low, high, 0, 1)[0:GROUP].astype(jnp.int32)
        return jnp.max(both[:, :LANES]), jnp.max(both[:, LANES:])

    extent, skew = numbers(to_core, to_chip)
    next_extent, next_skew = numbers(chip, core)
    for c in range(chans):
        rows[c, 0:reach, :] = pick(core, chip, c, 1)[strip_rows - reach :]
        turned = pltpu.roll(pick(core, chip, c, 0), skew, 1)
        top = pick(to_core, to_chip, c, 0)
        rows[c, reach : reach + strip_rows, :] = jnp.where(tall < extent, 0.5 * (top + turned), top)
        rows[c, reach + strip_rows : reach + row_count, :] = pick(to_chip, to_core, c, 1)
        turned = pltpu.roll(pick(to_chip, to_core, c, 0), next_skew, 1)
        top = pick(chip, core, c, 0)
        after = jnp.where(tall < next_extent, 0.5 * (top + turned), top)
        rows[c, reach + row_count : row_count + 2 * reach, :] = after[0:reach]
        whole = rows[c, 0 : row_count + 2 * reach, :]
        left, right = whole[:, :LANES], whole[:, LANES:]
        left_up, left_down = pltpu.roll(left, edge, 1), pltpu.roll(left, LANES - edge, 1)
        right_up, right_down = pltpu.roll(right, edge, 1), pltpu.roll(right, LANES - edge, 1)
        low, high = lane < edge, lane < LANES - edge
        cut = (
            jnp.where(low, 0.0, left_up),
            jnp.where(high, left_down, right_down),
            jnp.where(low, left_up, right_up),
            jnp.where(high, right_down, 0.0),
        )
        for b in range(row_blocks):
            for j in range(blocks):
                start = b * block_rows
                windows[(c * row_blocks + b) * blocks + j] = cut[j][start : start + window_rows]


def split(value):
    high = value.astype(jnp.bfloat16)
    low = (value - high.astype(jnp.float32)).astype(jnp.bfloat16)
    return high, low


def stages(window_rows, lateral_half):
    def tiled(rows):
        return -(-rows // 16) * 16

    return [
        (tiled(window_rows - 2 * k * lateral_half), tiled(window_rows - 2 * (k + 1) * lateral_half))
        for k in range(2 * ITERS)
    ]


def bands_kernel(axial, lateral, along_z, along_x, *along_y, spans, share, order):
    width = lateral.shape[1]
    plane = lax.axis_index("plane")
    chan = jnp.int32(0)
    for place, owner in enumerate(order):
        chan = jnp.where(plane == owner, place // share, chan)
    taps = [lateral[chan, j] for j in range(width)]
    for j in range(axial.shape[1]):
        along_z[j] = jnp.full((GROUP, LANES), axial[chan, j], jnp.float32)
    offset = lax.broadcasted_iota(jnp.int32, (LANES, LANES), 0) - lax.broadcasted_iota(jnp.int32, (LANES, LANES), 1)

    def band(order, where, first):
        total = jnp.zeros((LANES, LANES), jnp.float32)
        for j in range(width):
            total = jnp.where(where == j + first, order[j], total)
        return split(total)

    for which in range(2):
        order = taps if which == 0 else taps[::-1]
        high, low = band(order, offset, -(width // 2))
        along_x[which, :LANES, :LANES] = high
        along_x[which, :LANES, LANES:] = low
        along_x[which, LANES:, :LANES] = high
        along_x[which, LANES:, LANES:] = jnp.zeros_like(low)
        high, low = band(order, -offset, 0)
        for k in range(which, len(spans), 2):
            read, written = spans[k]
            top, bottom = high[:written, :read], low[:written, :read]
            along_y[k][:written] = jnp.concatenate([top, top], axis=1)
            along_y[k][written:] = jnp.concatenate([bottom, jnp.zeros_like(bottom)], axis=1)


def deconvolve_kernel(windows, axial, x_bands, *refs, spans, lateral_half, out_rows, order, sent):
    y_bands, (result, blurred, estimate) = refs[: len(spans)], refs[len(spans) :]
    planes, window_rows, _ = windows.shape
    axial_half = axial.shape[0] // 2
    columns = [slice(q * LANES, (q + 1) * LANES) for q in range(planes)]

    def along_x(values, which):
        out = []
        for q in range(0, planes, 2):
            pair = jnp.concatenate(values[q : q + 2], axis=0)
            product = jnp.dot(jnp.concatenate(split(pair), axis=1), x_bands[which], preferred_element_type=jnp.float32)
            product = product[:, :LANES] + product[:, LANES:]
            out += [product[: pair.shape[0] // 2], product[pair.shape[0] // 2 :]]
        return out

    def along_y(k):
        read, written = spans[k]
        for q in range(0, planes, 2):
            pair = slice(q * LANES, (q + 2) * LANES)
            both = jnp.concatenate(split(blurred[0:read, pair]), axis=0)
            product = jnp.dot(y_bands[k][...], both, preferred_element_type=jnp.float32)
            blurred[0:written, pair] = product[:written] + product[written:]

    def along_z(values, flipped):
        out = []
        for p in range(planes):
            total = None
            for q in range(planes):
                at = (order[p] - order[q] if flipped else order[q] - order[p]) + axial_half
                if 0 <= at < 2 * axial_half + 1:
                    term = axial[at] * values[q]
                    total = term if total is None else total + term
            out.append(total)
        return out

    origin = 0
    for sweep in range(ITERS):
        read, written = spans[2 * sweep]
        if sweep == 0:
            values = along_x([windows[p] for p in range(planes)], 0)
            blurred[window_rows:read, :] = jnp.zeros((read - window_rows, planes * LANES), jnp.float32)
        else:
            values = along_x([estimate[0:read, columns[p]] for p in range(planes)], 0)
        for p in range(planes):
            blurred[0 : values[p].shape[0], columns[p]] = values[p]
        along_y(2 * sweep)
        origin += lateral_half
        for row in range(0, written, GROUP):
            at = slice(row, row + GROUP)
            mixed = along_z([blurred[at, columns[q]] for q in range(planes)], False)
            quotient = []
            for p in range(planes):
                joined = windows[p, row + origin : row + origin + GROUP, :]
                quotient.append(joined / jnp.where(joined > 0.0, mixed[p], 1.0))
            back = along_z(quotient, True)
            for p in range(planes):
                blurred[at, columns[p]] = back[p]
        read, written = spans[2 * sweep + 1]
        along_y(2 * sweep + 1)
        origin += lateral_half
        factor = along_x([blurred[0:written, columns[p]] for p in range(planes)], 1)
        for p in range(planes):
            if sweep == 0:
                before = windows[p, origin : origin + written, :]
            else:
                before = estimate[2 * lateral_half : 2 * lateral_half + written, columns[p]]
            estimate[0:written, columns[p]] = before * factor[p]
    half = out_rows // 2
    side = (LANES - LANES // 2) // 2
    lane = lax.broadcasted_iota(jnp.int32, (1, LANES), 1)
    for p in range(planes):
        first = pltpu.roll(estimate[0:half, columns[p]], LANES - side, 1)
        second = pltpu.roll(estimate[half:out_rows, columns[p]], side, 1)
        result[sent.index(order[p])] = jnp.where(lane < LANES // 2, first, second)


def unpack_kernel(received, out, *, blocks, row_blocks, order, sent):
    chans, _, row_count, voxels = out.shape
    half = received.shape[1]
    lane = lax.broadcasted_iota(jnp.int32, (1, LANES), 1)
    for c in range(chans):
        for b in range(row_blocks):
            for pair in range(blocks // 2):
                at = (c * row_blocks + b) * blocks + 2 * pair
                even, odd = received[sent.index(order[at])], received[sent.index(order[at + 1])]
                row = b * 2 * half
                columns = slice(pair * LANES, (pair + 1) * LANES)
                out[c, 0, row : row + half, columns] = jnp.where(lane < LANES // 2, even, pltpu.roll(odd, LANES // 2, 1))
                out[c, 0, row + half : row + 2 * half, columns] = jnp.where(lane < LANES // 2, pltpu.roll(even, LANES // 2, 1), odd)


def group_orders(planes):
    if planes == 8:
        return [5, 0, 4, 7, 1, 3, 2, 6], [5, 1, 0, 4, 7, 2, 3, 6]
    return list(range(planes)), list(range(planes))


def shards(observed, intersection_strip, axial_taps, lateral_taps, extents, section_skews):
    chans, _, row_count, voxels = observed.shape
    strip_rows = intersection_strip.shape[2]
    planes = lax.axis_size("plane")
    tiles = lax.axis_size("tile")
    order, sent = group_orders(planes)
    lateral_half = lateral_taps.shape[1] // 2
    reach = 2 * ITERS * lateral_half
    blocks = voxels // (LANES // 2)
    row_blocks = planes // (chans * blocks)
    out_rows = row_count // row_blocks
    window_rows = out_rows + 2 * reach
    cores = [(i, i ^ 1) for i in range(tiles)]
    chips = [pair for i in range(1, tiles - 1, 2) for pair in ((i, i + 1), (i + 1, i))]

    payload = jax.ShapeDtypeStruct((chans, 1, 2 * strip_rows, voxels), jnp.float32)
    to_core, to_chip = pl.pallas_call(
        payload_kernel,
        out_shape=(payload, payload),
        in_specs=[pl.BlockSpec(memory_space=pltpu.HBM)] * 2 + [in_smem()] * 2,
        out_specs=(in_vmem(), in_vmem()),
        scratch_shapes=[pltpu.SemaphoreType.DMA((3 * chans,))],
        compiler_params=params(),
        name="payload",
    )(*(pltpu.with_memory_space_constraint(array, pltpu.HBM) for array in (observed, intersection_strip)), extents, section_skews)
    chip = lax.ppermute(to_chip, "tile", chips)
    core = lax.ppermute(to_core, "tile", cores)
    spans = stages(window_rows, lateral_half)
    bands = pl.pallas_call(
        lambda *refs: bands_kernel(*refs, spans=spans, share=planes // chans, order=order),
        out_shape=[
            jax.ShapeDtypeStruct((axial_taps.shape[1], GROUP, LANES), jnp.float32),
            jax.ShapeDtypeStruct((2, 2 * LANES, 2 * LANES), jnp.bfloat16),
        ]
        + [jax.ShapeDtypeStruct((2 * written, 2 * read), jnp.bfloat16) for read, written in spans],
        in_specs=[in_smem()] * 2,
        out_specs=[in_vmem()] * (2 + len(spans)),
        cost_estimate=pl.CostEstimate(flops=1 << 20, bytes_accessed=1 << 20, transcendentals=0),
        compiler_params=params(),
        name="bands",
    )(axial_taps, lateral_taps)
    windows = pl.pallas_call(
        lambda *refs: pack_kernel(*refs, reach=reach, blocks=blocks, row_blocks=row_blocks),
        out_shape=jax.ShapeDtypeStruct((planes, window_rows, LANES), jnp.float32),
        in_specs=[in_vmem()] * 4 + [pl.BlockSpec(memory_space=pl.ANY)],
        out_specs=in_vmem(),
        scratch_shapes=[pltpu.VMEM((chans, row_count + 2 * reach, voxels), jnp.float32)],
        compiler_params=params(),
        name="pack",
    )(to_core, to_chip, core, chip, bands[0])
    windows = lax.all_to_all(windows, "plane", 0, 0, axis_index_groups=[order], tiled=True)

    result = pl.pallas_call(
        lambda *refs: deconvolve_kernel(*refs, spans=spans, lateral_half=lateral_half, out_rows=out_rows, order=order, sent=sent),
        out_shape=jax.ShapeDtypeStruct((planes, out_rows // 2, LANES), jnp.float32),
        in_specs=[in_vmem()] * (3 + len(spans)),
        out_specs=in_vmem(),
        scratch_shapes=[
            pltpu.VMEM((spans[0][0], planes * LANES), jnp.float32),
            pltpu.VMEM((spans[1][1], planes * LANES), jnp.float32),
        ],
        compiler_params=params(),
        name="deconvolve",
    )(windows, *bands)
    received = lax.all_to_all(result, "plane", 0, 0, axis_index_groups=[sent], tiled=True)
    return pl.pallas_call(
        lambda *refs: unpack_kernel(*refs, blocks=blocks, row_blocks=row_blocks, order=order, sent=sent),
        out_shape=jax.ShapeDtypeStruct(observed.shape, jnp.float32),
        in_specs=[in_vmem()],
        out_specs=in_vmem(),
        compiler_params=params(),
        name="unpack",
    )(received)


def solution(mesh):
    in_specs = (
        P(None, "plane", "tile", None),
        P(None, "plane", "tile", None),
        P(),
        P(),
        P("tile"),
        P("tile"),
    )
    out_specs = P(None, "plane", "tile", None)
    return jax.shard_map(shards, mesh=mesh, in_specs=in_specs, out_specs=out_specs, check_vma=False)
```

```python
import jax
import jax.numpy as jnp
from jax import lax
from jax.experimental import pallas as pl
from jax.experimental.pallas import tpu as pltpu
from jax.sharding import PartitionSpec as P

ITERS = 2
LANES = 128
GROUP = 8
VMEM_LIMIT = 48 * 1024 * 1024


def params():
    return pltpu.CompilerParams(vmem_limit_bytes=VMEM_LIMIT)


def in_vmem():
    return pl.BlockSpec(memory_space=pltpu.VMEM)


def in_smem():
    return pl.BlockSpec(memory_space=pltpu.SMEM)


def payload_kernel(own, strip, extents, skews, to_core, to_chip, sems):
    strip_rows = strip.shape[2]
    tile = lax.axis_index("tile")
    low, high = slice(0, strip_rows), slice(strip_rows, 2 * strip_rows)

    def fill(up, down):
        pieces = []
        for c in range(strip.shape[0]):
            pieces += [
                (strip.at[c], up.at[c, :, low, :]),
                (own.at[c, :, own.shape[2] - strip_rows :, :], up.at[c, :, high, :]),
                (own.at[c, :, low, :], down.at[c, :, low, :]),
            ]
        copies = [pltpu.make_async_copy(source, target, sems.at[i]) for i, (source, target) in enumerate(pieces)]
        for copy in copies:
            copy.start()
        extent = jnp.where(tile == 0, 0, extents[0])
        column = lax.broadcasted_iota(jnp.int32, strip.shape, 3)
        down[:, :, high, :] = jnp.where(column < LANES, extent, skews[0]).astype(jnp.float32)
        for copy in copies:
            copy.wait()

    @pl.when(tile % 2 == 1)
    def _():
        fill(to_chip, to_core)

    @pl.when(tile % 2 == 0)
    def _():
        fill(to_core, to_chip)


def pack_kernel(to_core, to_chip, core, chip, _, windows, rows, *, reach, blocks, row_blocks):
    chans, _, row_count, voxels = core.shape
    strip_rows = row_count // 2
    lane = lax.broadcasted_iota(jnp.int32, (1, LANES), 1)
    tall = lax.broadcasted_iota(jnp.int32, (strip_rows, voxels), 0)
    edge = LANES // 4
    block_rows = row_count // row_blocks
    window_rows = block_rows + 2 * reach
    lower = lax.axis_index("tile") % 2 == 1

    def pick(low, high, c, part):
        at = slice(part * strip_rows, (part + 1) * strip_rows)
        return jnp.where(lower, low[c, 0, at, :], high[c, 0, at, :])

    def numbers(low, high):
        both = pick(low, high, 0, 1)[0:GROUP].astype(jnp.int32)
        return jnp.max(both[:, :LANES]), jnp.max(both[:, LANES:])

    extent, skew = numbers(to_core, to_chip)
    next_extent, next_skew = numbers(chip, core)
    for c in range(chans):
        rows[c, 0:reach, :] = pick(core, chip, c, 1)[strip_rows - reach :]
        turned = pltpu.roll(pick(core, chip, c, 0), skew, 1)
        top = pick(to_core, to_chip, c, 0)
        rows[c, reach : reach + strip_rows, :] = jnp.where(tall < extent, 0.5 * (top + turned), top)
        rows[c, reach + strip_rows : reach + row_count, :] = pick(to_chip, to_core, c, 1)
        turned = pltpu.roll(pick(to_chip, to_core, c, 0), next_skew, 1)
        top = pick(chip, core, c, 0)
        after = jnp.where(tall < next_extent, 0.5 * (top + turned), top)
        rows[c, reach + row_count : row_count + 2 * reach, :] = after[0:reach]
        whole = rows[c, 0 : row_count + 2 * reach, :]
        left, right = whole[:, :LANES], whole[:, LANES:]
        left_up, left_down = pltpu.roll(left, edge, 1), pltpu.roll(left, LANES - edge, 1)
        right_up, right_down = pltpu.roll(right, edge, 1), pltpu.roll(right, LANES - edge, 1)
        low, high = lane < edge, lane < LANES - edge
        cut = (
            jnp.where(low, 0.0, left_up),
            jnp.where(high, left_down, right_down),
            jnp.where(low, left_up, right_up),
            jnp.where(high, right_down, 0.0),
        )
        for b in range(row_blocks):
            for j in range(blocks):
                start = b * block_rows
                windows[(c * row_blocks + b) * blocks + j] = cut[j][start : start + window_rows]


def split(value):
    high = value.astype(jnp.bfloat16)
    low = (value - high.astype(jnp.float32)).astype(jnp.bfloat16)
    return high, low


def stages(window_rows, lateral_half):
    def tiled(rows):
        return -(-rows // 16) * 16

    return [
        (tiled(window_rows - 2 * k * lateral_half), tiled(window_rows - 2 * (k + 1) * lateral_half))
        for k in range(2 * ITERS)
    ]


def bands_kernel(axial, lateral, along_z, along_x, *along_y, spans, share, order):
    width = lateral.shape[1]
    plane = lax.axis_index("plane")
    chan = jnp.int32(0)
    for place, owner in enumerate(order):
        chan = jnp.where(plane == owner, place // share, chan)
    taps = [lateral[chan, j] for j in range(width)]
    for j in range(axial.shape[1]):
        along_z[j] = jnp.full((GROUP, LANES), axial[chan, j], jnp.float32)
    offset = lax.broadcasted_iota(jnp.int32, (LANES, LANES), 0) - lax.broadcasted_iota(jnp.int32, (LANES, LANES), 1)

    def band(order, where, first):
        total = jnp.zeros((LANES, LANES), jnp.float32)
        for j in range(width):
            total = jnp.where(where == j + first, order[j], total)
        return split(total)

    for which in range(2):
        order = taps if which == 0 else taps[::-1]
        high, low = band(order, offset, -(width // 2))
        along_x[which, :LANES, :LANES] = high
        along_x[which, :LANES, LANES:] = low
        along_x[which, LANES:, :LANES] = high
        along_x[which, LANES:, LANES:] = jnp.zeros_like(low)
        high, low = band(order, -offset, 0)
        for k in range(which, len(spans), 2):
            read, written = spans[k]
            top, bottom = high[:written, :read], low[:written, :read]
            along_y[k][:written] = jnp.concatenate([top, top], axis=1)
            along_y[k][written:] = jnp.concatenate([bottom, jnp.zeros_like(bottom)], axis=1)


def deconvolve_kernel(windows, axial, x_bands, *refs, spans, lateral_half, out_rows, order, sent):
    y_bands, (result, blurred, estimate) = refs[: len(spans)], refs[len(spans) :]
    planes, window_rows, _ = windows.shape
    axial_half = axial.shape[0] // 2
    columns = [slice(q * LANES, (q + 1) * LANES) for q in range(planes)]

    def along_x(values, which):
        rows = values[0].shape[0]
        both = jnp.concatenate(split(jnp.concatenate(values, axis=0)), axis=1)
        product = jnp.dot(both, x_bands[which], preferred_element_type=jnp.float32)
        product = product[:, :LANES] + product[:, LANES:]
        return [product[q * rows : (q + 1) * rows] for q in range(planes)]

    def along_y(k):
        read, written = spans[k]
        both = jnp.concatenate(split(blurred[0:read, :]), axis=0)
        product = jnp.dot(y_bands[k][...], both, preferred_element_type=jnp.float32)
        blurred[0:written, :] = product[:written] + product[written:]

    def along_z(values, flipped):
        out = []
        for p in range(planes):
            total = None
            for q in range(planes):
                at = (order[p] - order[q] if flipped else order[q] - order[p]) + axial_half
                if 0 <= at < 2 * axial_half + 1:
                    term = axial[at] * values[q]
                    total = term if total is None else total + term
            out.append(total)
        return out

    origin = 0
    for sweep in range(ITERS):
        read, written = spans[2 * sweep]
        if sweep == 0:
            values = along_x([windows[p] for p in range(planes)], 0)
            blurred[window_rows:read, :] = jnp.zeros((read - window_rows, planes * LANES), jnp.float32)
        else:
            values = along_x([estimate[0:read, columns[p]] for p in range(planes)], 0)
        for p in range(planes):
            blurred[0 : values[p].shape[0], columns[p]] = values[p]
        along_y(2 * sweep)
        origin += lateral_half
        for row in range(0, written, GROUP):
            at = slice(row, row + GROUP)
            mixed = along_z([blurred[at, columns[q]] for q in range(planes)], False)
            quotient = []
            for p in range(planes):
                joined = windows[p, row + origin : row + origin + GROUP, :]
                quotient.append(joined / jnp.where(joined > 0.0, mixed[p], 1.0))
            back = along_z(quotient, True)
            for p in range(planes):
                blurred[at, columns[p]] = back[p]
        read, written = spans[2 * sweep + 1]
        along_y(2 * sweep + 1)
        origin += lateral_half
        factor = along_x([blurred[0:written, columns[p]] for p in range(planes)], 1)
        for p in range(planes):
            if sweep == 0:
                before = windows[p, origin : origin + written, :]
            else:
                before = estimate[2 * lateral_half : 2 * lateral_half + written, columns[p]]
            estimate[0:written, columns[p]] = before * factor[p]
    half = out_rows // 2
    side = (LANES - LANES // 2) // 2
    lane = lax.broadcasted_iota(jnp.int32, (1, LANES), 1)
    for p in range(planes):
        first = pltpu.roll(estimate[0:half, columns[p]], LANES - side, 1)
        second = pltpu.roll(estimate[half:out_rows, columns[p]], side, 1)
        result[sent.index(order[p])] = jnp.where(lane < LANES // 2, first, second)


def unpack_kernel(received, out, *, blocks, row_blocks, order, sent):
    chans, _, row_count, voxels = out.shape
    half = received.shape[1]
    lane = lax.broadcasted_iota(jnp.int32, (1, LANES), 1)
    for c in range(chans):
        for b in range(row_blocks):
            for pair in range(blocks // 2):
                at = (c * row_blocks + b) * blocks + 2 * pair
                even, odd = received[sent.index(order[at])], received[sent.index(order[at + 1])]
                row = b * 2 * half
                columns = slice(pair * LANES, (pair + 1) * LANES)
                out[c, 0, row : row + half, columns] = jnp.where(lane < LANES // 2, even, pltpu.roll(odd, LANES // 2, 1))
                out[c, 0, row + half : row + 2 * half, columns] = jnp.where(lane < LANES // 2, pltpu.roll(even, LANES // 2, 1), odd)


def group_orders(planes):
    if planes == 8:
        return [5, 0, 4, 7, 3, 1, 2, 6], [5, 1, 0, 4, 7, 2, 3, 6]
    return list(range(planes)), list(range(planes))


def shards(observed, intersection_strip, axial_taps, lateral_taps, extents, section_skews):
    chans, _, row_count, voxels = observed.shape
    strip_rows = intersection_strip.shape[2]
    planes = lax.axis_size("plane")
    tiles = lax.axis_size("tile")
    order, sent = group_orders(planes)
    lateral_half = lateral_taps.shape[1] // 2
    reach = 2 * ITERS * lateral_half
    blocks = voxels // (LANES // 2)
    row_blocks = planes // (chans * blocks)
    out_rows = row_count // row_blocks
    window_rows = out_rows + 2 * reach
    cores = [(i, i ^ 1) for i in range(tiles)]
    chips = [pair for i in range(1, tiles - 1, 2) for pair in ((i, i + 1), (i + 1, i))]

    payload = jax.ShapeDtypeStruct((chans, 1, 2 * strip_rows, voxels), jnp.float32)
    to_core, to_chip = pl.pallas_call(
        payload_kernel,
        out_shape=(payload, payload),
        in_specs=[pl.BlockSpec(memory_space=pltpu.HBM)] * 2 + [in_smem()] * 2,
        out_specs=(in_vmem(), in_vmem()),
        scratch_shapes=[pltpu.SemaphoreType.DMA((3 * chans,))],
        compiler_params=params(),
        name="payload",
    )(*(pltpu.with_memory_space_constraint(array, pltpu.HBM) for array in (observed, intersection_strip)), extents, section_skews)
    chip = lax.ppermute(to_chip, "tile", chips)
    core = lax.ppermute(to_core, "tile", cores)
    spans = stages(window_rows, lateral_half)
    bands = pl.pallas_call(
        lambda *refs: bands_kernel(*refs, spans=spans, share=planes // chans, order=order),
        out_shape=[
            jax.ShapeDtypeStruct((axial_taps.shape[1], GROUP, LANES), jnp.float32),
            jax.ShapeDtypeStruct((2, 2 * LANES, 2 * LANES), jnp.bfloat16),
        ]
        + [jax.ShapeDtypeStruct((2 * written, 2 * read), jnp.bfloat16) for read, written in spans],
        in_specs=[in_smem()] * 2,
        out_specs=[in_vmem()] * (2 + len(spans)),
        cost_estimate=pl.CostEstimate(flops=1 << 20, bytes_accessed=1 << 20, transcendentals=0),
        compiler_params=params(),
        name="bands",
    )(axial_taps, lateral_taps)
    windows = pl.pallas_call(
        lambda *refs: pack_kernel(*refs, reach=reach, blocks=blocks, row_blocks=row_blocks),
        out_shape=jax.ShapeDtypeStruct((planes, window_rows, LANES), jnp.float32),
        in_specs=[in_vmem()] * 4 + [pl.BlockSpec(memory_space=pl.ANY)],
        out_specs=in_vmem(),
        scratch_shapes=[pltpu.VMEM((chans, row_count + 2 * reach, voxels), jnp.float32)],
        compiler_params=params(),
        name="pack",
    )(to_core, to_chip, core, chip, bands[0])
    windows = lax.all_to_all(windows, "plane", 0, 0, axis_index_groups=[order], tiled=True)

    result = pl.pallas_call(
        lambda *refs: deconvolve_kernel(*refs, spans=spans, lateral_half=lateral_half, out_rows=out_rows, order=order, sent=sent),
        out_shape=jax.ShapeDtypeStruct((planes, out_rows // 2, LANES), jnp.float32),
        in_specs=[in_vmem()] * (3 + len(spans)),
        out_specs=in_vmem(),
        scratch_shapes=[
            pltpu.VMEM((spans[0][0], planes * LANES), jnp.float32),
            pltpu.VMEM((spans[1][1], planes * LANES), jnp.float32),
        ],
        compiler_params=params(),
        name="deconvolve",
    )(windows, *bands)
    received = lax.all_to_all(result, "plane", 0, 0, axis_index_groups=[sent], tiled=True)
    return pl.pallas_call(
        lambda *refs: unpack_kernel(*refs, blocks=blocks, row_blocks=row_blocks, order=order, sent=sent),
        out_shape=jax.ShapeDtypeStruct(observed.shape, jnp.float32),
        in_specs=[in_vmem()],
        out_specs=in_vmem(),
        compiler_params=params(),
        name="unpack",
    )(received)


def solution(mesh):
    in_specs = (
        P(None, "plane", "tile", None),
        P(None, "plane", "tile", None),
        P(),
        P(),
        P("tile"),
        P("tile"),
    )
    out_specs = P(None, "plane", "tile", None)
    return jax.shard_map(shards, mesh=mesh, in_specs=in_specs, out_specs=out_specs, check_vma=False)
```
